32 devices in a mesh: narrow: 4 (over x, core), wide: 8 (over z, y).
Axes of the slice: x: 2, y: 2, z: 4, core: 2. Of those that a mesh axis runs over, the one named last changes fastest.
Arguments:
- inputs: bfloat16 [32, 2304], P('wide', 'narrow'), may hold values from -6 to 6
- decoder_bias: float32 [2304], replicated, may hold values from -3 to 3
- preactivations: bfloat16 [32, 8192], P(None, ('narrow', 'wide')), may hold values from -6 to 6
- decoder_weight: bfloat16 [8192, 2304], P(('narrow', 'wide')), may hold values from -0.125 to 0.125
Outputs:
- grad_encoder: bfloat16 [2304, 8192], P(None, ('narrow', 'wide'))
- grad_decoder: bfloat16 [8192, 2304], P(('narrow', 'wide'))
The draws below stay inside these ranges and needn't reach their ends.
All inputs are finite; a program needn't handle non-finite values.
Results may differ from the reference program's by a relative error of at most 0.0053.
Values may be sent and summed in bfloat16 or wider, within the bound.
A program may use at most 64 MiB of HBM per device.

```python
import jax
import jax.numpy as jnp

D = 2304
FEATURES = 8192
ROWS = 32


def raised(result, stream_key, source, target, parts, factor):
    def block_of(position):
        return (jnp.arange(result.shape[position]) // (result.shape[position] // parts)).reshape((-1,) + (1,) * (result.ndim - 1 - position))

    one_side = jax.random.permutation(stream_key, parts)[block_of(target)]
    second = (block_of(target) + parts // 2) % parts
    return jnp.where((block_of(source) == one_side) | (block_of(source) == second), factor * result, result)


def block_scale(key, extent, cuts, low, largest):
    def one(dim, parts):
        steps = jax.random.uniform(jax.random.fold_in(jax.random.fold_in(key, 6), dim), (parts,), jnp.float32, low / len(cuts), largest / len(cuts))
        return jnp.repeat(jnp.exp(steps), extent[dim] // parts).reshape((-1,) + (1,) * (len(extent) - dim - 1))

    gain = one(*cuts[0])
    for cut in cuts[1:]:
        gain = gain * one(*cut)
    return gain


def bell_draw(stream_key, dims, spread, limit, pieces=(), kind=jnp.bfloat16):
    values = spread * jax.random.normal(stream_key, dims, jnp.float32)
    if pieces:
        values = values * block_scale(stream_key, dims, pieces, -0.22, 0.18)
    return jnp.clip(values, -limit, limit).astype(kind)


def gaussian_with(stream_key, extent, width, most, cuts, heavy, kind=jnp.bfloat16):
    drawn = width * jax.random.normal(stream_key, extent, jnp.float32)
    if cuts:
        drawn = drawn * block_scale(stream_key, extent, cuts, -0.22, 0.18)
    return jnp.clip(raised(drawn, jax.random.fold_in(stream_key, 3), *heavy), -most, most).astype(kind)


def setup_inputs(seed: int = 0) -> dict:
    keys = jax.random.split(jax.random.key(seed), 5)
    inputs = bell_draw(keys[0], (ROWS, D), 1.0, 6.0, ((0, 8), (1, 4)))
    decoder_bias = bell_draw(keys[1], (D,), 0.5, 3.0, (), jnp.float32)
    preactivations = bell_draw(keys[2], (ROWS, FEATURES), 1.0, 6.0, ((1, 32),))
    decoder_weight = gaussian_with(keys[3], (FEATURES, D), FEATURES ** -0.5, 0.125, ((0, 32),), (0, 1, 32, 2.75))
    return dict(inputs=inputs, decoder_bias=decoder_bias, preactivations=preactivations, decoder_weight=decoder_weight)


def reference(inputs, decoder_bias, preactivations, decoder_weight):
    hidden = jnp.maximum(preactivations, jnp.zeros_like(preactivations))
    recon = jnp.dot(hidden, decoder_weight, preferred_element_type=jnp.float32) + decoder_bias
    residual = (recon - inputs.astype(jnp.float32)).astype(jnp.bfloat16)
    centered = (inputs.astype(jnp.float32) - decoder_bias).astype(jnp.bfloat16)
    grad_decoder = jnp.dot(hidden.T, residual, preferred_element_type=jnp.float32).astype(jnp.bfloat16)
    backward = jnp.dot(residual, decoder_weight.T, preferred_element_type=jnp.float32)
    masked = jnp.where(preactivations > 0, backward, jnp.zeros_like(backward)).astype(jnp.bfloat16)
    grad_encoder = jnp.dot(centered.T, masked, preferred_element_type=jnp.float32).astype(jnp.bfloat16)
    return grad_encoder, grad_decoder
```

```python
import functools

import jax
import jax.numpy as jnp
from jax import lax
from jax.experimental import pallas as pl
from jax.experimental.pallas import tpu as pltpu
from jax.sharding import PartitionSpec as P

MESH = pl.DeviceIdType.MESH
LANES = 128
BF16 = jnp.bfloat16
F32 = jnp.float32


def each(low, high, body):
    if high - low <= 16:
        for i in range(low, high):
            body(i)
    else:
        lax.fori_loop(low, high, lambda i, _: (body(i), 0)[1], 0)


def wait_bytes(ref, sem):
    pltpu.make_async_copy(ref, ref, sem).wait()


def exchange(narrow, wide, pieces, in_ref, bias_ref, pre_ref, w_hbm, resid_ref, cent_ref,
             w_ref, blocks, whole, mine, theirs, part, landed, res,
             w_sem, in_send, in_recv, inx_send, inx_recv, px_send, px_recv,
             part_send, part_recv, res_send, res_recv, rx_send, rx_recv):
    n, w = lax.axis_index("narrow"), lax.axis_index("wide")
    core, chip = n % 2, (n // 2) * wide + w
    other = 1 - core
    chips = (narrow // 2) * wide
    rows, width = whole.shape
    half = width // 2
    cols = half // LANES
    tall = part.shape[1]
    block_rows, block_cols = in_ref.shape
    stride, shift = chips // pieces, core * (chips // 2)

    def device(c):
        return {"narrow": (c // wide) * 2 + core, "wide": c % wide}

    partner = {"narrow": (n // 2) * 2 + other, "wide": w}
    place = (chip + chips - shift) % chips
    owner = (place % stride == 0) & (place // stride < pieces)
    own = lax.min(place // stride, pieces - 1)

    barrier = pltpu.get_barrier_semaphore()
    pl.semaphore_signal(barrier, inc=1, device_id=partner, device_id_type=MESH)
    each(1, chips, lambda i: pl.semaphore_signal(
        barrier, inc=1, device_id=device((chip + i) % chips), device_id_type=MESH))

    def load(h, slot):
        span = pl.ds(pl.multiple_of(h * half, LANES), half)
        return pltpu.make_async_copy(w_hbm.at[:, span], w_ref.at[slot], w_sem.at[slot])

    load(other, 0).start()
    load(core, 1).start()
    blocks[core, chip] = in_ref[...]
    pl.semaphore_wait(barrier, chips)

    def send_block(i):
        pltpu.make_async_remote_copy(
            src_ref=in_ref, dst_ref=blocks.at[core, chip], send_sem=in_send, recv_sem=in_recv,
            device_id=device((chip + i) % chips), device_id_type=MESH).start()

    each(1, chips, send_block)

    hidden = jnp.maximum(pre_ref[...], jnp.zeros_like(pre_ref))
    load(other, 0).wait()
    mine[...] = jnp.dot(hidden, w_ref[0], preferred_element_type=F32)
    swap = pltpu.make_async_remote_copy(
        src_ref=mine, dst_ref=theirs, send_sem=px_send, recv_sem=px_recv,
        device_id=partner, device_id_type=MESH)
    swap.start()
    load(core, 1).wait()
    total = jnp.dot(hidden, w_ref[1], preferred_element_type=F32)
    swap.wait()
    total = (total + theirs[...]).astype(BF16)
    for k in range(pieces):
        q, j = k // cols, k % cols
        part[k] = total[q * tall:(q + 1) * tall, j * LANES:(j + 1) * LANES]

    def send_part(i):
        k = (chip + i) % pieces
        to = (k * stride + shift) % chips

        @pl.when(to != chip)
        def _():
            pltpu.make_async_remote_copy(
                src_ref=part.at[k], dst_ref=landed.at[chip], send_sem=part_send, recv_sem=part_recv,
                device_id=device(to), device_id_type=MESH).start()

    each(0, pieces, send_part)

    wait_bytes(blocks.at[core, pl.ds(0, chips - 1)], in_recv)
    forward = pltpu.make_async_remote_copy(
        src_ref=blocks.at[core], dst_ref=blocks.at[core], send_sem=inx_send, recv_sem=inx_recv,
        device_id=partner, device_id_type=MESH)
    forward.start()
    wait_bytes(blocks.at[core, pl.ds(0, chips - 1)], in_send)
    forward.wait()
    for a in range(narrow):
        for b in range(wide):
            whole[b * block_rows:(b + 1) * block_rows, a * block_cols:(a + 1) * block_cols] = (
                blocks[a % 2, (a // 2) * wide + b].astype(F32))
    cent_ref[...] = (whole[...] - bias_ref[...]).astype(BF16)

    @pl.when(owner)
    def _():
        landed[chip] = part[own]
        wait_bytes(landed.at[pl.ds(0, chips - 1)], part_recv)
        reduced = jnp.sum(landed[...].astype(F32), axis=0)
        at = pl.ds(pl.multiple_of(core * half + (own % cols) * LANES, LANES), LANES)
        down = pl.ds(pl.multiple_of((own // cols) * tall, 16), tall)
        res[core, own] = (reduced + bias_ref[:, at] - whole[down, at]).astype(BF16)

        def send_res(i):
            pltpu.make_async_remote_copy(
                src_ref=res.at[core, own], dst_ref=res.at[core, own], send_sem=res_send,
                recv_sem=res_recv, device_id=device((chip + i) % chips),
                device_id_type=MESH).start()

        each(1, chips, send_res)
        wait_bytes(part.at[pl.ds(0, pieces - 1)], part_send)
        wait_bytes(res.at[core, pl.ds(0, pieces - 1)], res_recv)

    @pl.when(jnp.logical_not(owner))
    def _():
        wait_bytes(part, part_send)
        wait_bytes(res.at[core], res_recv)

    last = pltpu.make_async_remote_copy(
        src_ref=res.at[core], dst_ref=res.at[core], send_sem=rx_send, recv_sem=rx_recv,
        device_id=partner, device_id_type=MESH)
    last.start()

    @pl.when(owner)
    def _():
        wait_bytes(landed.at[pl.ds(0, chips - 1)], res_send)

    last.wait()
    for h in range(2):
        for k in range(pieces):
            q, j = k // cols, k % cols
            at = h * half + j * LANES
            resid_ref[q * tall:(q + 1) * tall, at:at + LANES] = res[h, k]


def gradients(pre_ref, resid_ref, cent_ref, w_hbm, enc_hbm, dec_hbm, w_ref, enc, dec, w_sem, enc_sem, dec_sem):
    load = pltpu.make_async_copy(w_hbm, w_ref, w_sem)
    load.start()
    width = resid_ref.shape[1]
    cuts = dec_sem.shape[0]
    step = width // cuts
    pre = pre_ref[...]
    hidden = jnp.maximum(pre, jnp.zeros_like(pre))
    rows_first = (((0,), (0,)), ((), ()))
    copies = []
    for i in range(cuts):
        span = slice(i * step, (i + 1) * step)
        dec[:, span] = lax.dot_general(
            hidden, resid_ref[:, span], rows_first, preferred_element_type=F32).astype(BF16)
        copies.append(pltpu.make_async_copy(dec.at[:, span], dec_hbm.at[:, span], dec_sem.at[i]))
        copies[-1].start()
    load.wait()
    backward = lax.dot_general(
        resid_ref[...], w_ref[...], (((1,), (1,)), ((), ())), preferred_element_type=F32)
    masked = jnp.where(pre.astype(F32) > 0, backward, 0.0).astype(BF16)
    for i in range(cuts):
        span = slice(i * step, (i + 1) * step)
        enc[span, :] = lax.dot_general(
            cent_ref[:, span], masked, rows_first, preferred_element_type=F32).astype(BF16)
        copies.append(pltpu.make_async_copy(enc.at[span, :], enc_hbm.at[span, :], enc_sem.at[i]))
        copies[-1].start()
    for copy in copies:
        copy.wait()


def shards(narrow, wide, inputs, decoder_bias, preactivations, decoder_weight):
    rows, features = preactivations.shape
    width = decoder_weight.shape[1]
    half, chips = width // 2, (narrow // 2) * wide
    cols = half // LANES
    groups = 1
    while cols * groups * 2 <= chips and rows % (groups * 2 * 16) == 0:
        groups *= 2
    pieces, tall = cols * groups, rows // groups
    vmem, hbm = pl.BlockSpec(memory_space=pltpu.VMEM), pl.BlockSpec(memory_space=pl.ANY)
    dma = pltpu.SemaphoreType.DMA
    whole = jax.ShapeDtypeStruct((rows, width), BF16)
    resid, centered = pl.pallas_call(
        functools.partial(exchange, narrow, wide, pieces),
        out_shape=(whole, whole),
        in_specs=[vmem, vmem, vmem, hbm],
        out_specs=(vmem, vmem),
        scratch_shapes=[
            pltpu.VMEM((2, features, half), BF16),
            pltpu.VMEM((2, chips) + inputs.shape, BF16),
            pltpu.VMEM((rows, width), F32),
            pltpu.VMEM((rows, half), F32),
            pltpu.VMEM((rows, half), F32),
            pltpu.VMEM((pieces, tall, LANES), BF16),
            pltpu.VMEM((chips, tall, LANES), BF16),
            pltpu.VMEM((2, pieces, tall, LANES), BF16),
            dma((2,)),
        ] + [dma] * 12,
        compiler_params=pltpu.CompilerParams(
            collective_id=0, has_side_effects=True, vmem_limit_bytes=32 * 2**20),
        name="exchange",
    )(inputs, decoder_bias.reshape(1, width), preactivations, decoder_weight)
    cuts = 3
    return pl.pallas_call(
        gradients,
        out_shape=(jax.ShapeDtypeStruct((width, features), BF16),
                   jax.ShapeDtypeStruct((features, width), BF16)),
        in_specs=[vmem, vmem, vmem, hbm],
        out_specs=(hbm, hbm),
        scratch_shapes=[
            pltpu.VMEM((features, width), BF16),
            pltpu.VMEM((width, features), BF16),
            pltpu.VMEM((features, width), BF16),
            dma, dma((cuts,)), dma((cuts,)),
        ],
        compiler_params=pltpu.CompilerParams(vmem_limit_bytes=32 * 2**20),
        name="gradients",
    )(preactivations, resid, centered, decoder_weight)


def solution(mesh):
    placed = (P("wide", "narrow"), P(), P(None, ("narrow", "wide")), P(("narrow", "wide"), None))
    return jax.shard_map(
        functools.partial(shards, mesh.shape["narrow"], mesh.shape["wide"]),
        mesh=mesh,
        in_specs=placed,
        out_specs=(P(None, ("narrow", "wide")), P(("narrow", "wide"), None)),
        check_vma=False,
    )
```

```python
import functools

import jax
import jax.numpy as jnp
from jax import lax
from jax.experimental import pallas as pl
from jax.experimental.pallas import tpu as pltpu
from jax.sharding import PartitionSpec as P

MESH = pl.DeviceIdType.MESH
LANES = 128
BF16 = jnp.bfloat16
F32 = jnp.float32


def each(low, high, body):
    if high - low <= 16:
        for i in range(low, high):
            body(i)
    else:
        lax.fori_loop(low, high, lambda i, _: (body(i), 0)[1], 0)


def wait_bytes(ref, sem):
    pltpu.make_async_copy(ref, ref, sem).wait()


def exchange(narrow, wide, pieces, in_hbm, bias_hbm, pre_hbm, w_hbm, resid_ref, cent_ref, hid_ref,
             w_ref, in_ref, pre_ref, flat, bias_ref, band, blocks, whole, mine, theirs, part, landed, res,
             w_sem, in_sem, pre_sem, bias_sem, in_send, in_recv, inx_send, inx_recv, px_send, px_recv,
             part_send, part_recv, res_send, res_recv, rx_send, rx_recv):
    n, w = lax.axis_index("narrow"), lax.axis_index("wide")
    core, chip = n % 2, (n // 2) * wide + w
    other = 1 - core
    chips = (narrow // 2) * wide
    rows, width = whole.shape
    half = width // 2
    cols = half // LANES
    tall = part.shape[1]
    block_rows, block_cols = in_ref.shape
    stride, shift = chips // pieces, core * (chips // 2)

    def device(c):
        return {"narrow": (c // wide) * 2 + core, "wide": c % wide}

    partner = {"narrow": (n // 2) * 2 + other, "wide": w}
    place = (chip + chips - shift) % chips
    owner = (place % stride == 0) & (place // stride < pieces)
    own = lax.min(place // stride, pieces - 1)

    def columns(h):
        return pl.ds(pl.multiple_of(h * half, LANES), half)

    def load(h, slot):
        return pltpu.make_async_copy(w_hbm.at[:, columns(h)], w_ref.at[slot], w_sem.at[slot])

    small = [pltpu.make_async_copy(in_hbm, in_ref, in_sem),
             pltpu.make_async_copy(pre_hbm, pre_ref, pre_sem),
             pltpu.make_async_copy(bias_hbm, flat, bias_sem)]
    for copy in small:
        copy.start()
    load(other, 0).start()
    load(core, 1).start()

    barrier = pltpu.get_barrier_semaphore()
    pl.semaphore_signal(barrier, inc=1, device_id=partner, device_id_type=MESH)
    each(1, chips, lambda i: pl.semaphore_signal(
        barrier, inc=1, device_id=device((chip + i) % chips), device_id_type=MESH))

    for copy in small:
        copy.wait()
    block = in_ref[...]
    blocks[core, chip] = block
    bias_ref[...] = flat[...].reshape(1, width)
    for a in range(narrow):
        for b in range(8 // block_rows):
            band[b * block_rows:(b + 1) * block_rows, a * block_cols:(a + 1) * block_cols] = block.astype(F32)

    def placed(h):
        repeated = jnp.concatenate([band[:, columns(h)]] * (rows // 8), axis=0)
        row = lax.broadcasted_iota(jnp.int32, (rows, half), 0) - w * block_rows
        col = lax.broadcasted_iota(jnp.int32, (rows, half), 1) + (h * half - n * block_cols)
        inside = (row >= 0) & (row < block_rows) & (col >= 0) & (col < block_cols)
        return jnp.where(inside, repeated, 0.0)

    hidden = jnp.maximum(pre_ref[...], jnp.zeros_like(pre_ref))
    load(other, 0).wait()
    mine[...] = jnp.dot(hidden, w_ref[0], preferred_element_type=F32) - placed(other)
    pl.semaphore_wait(barrier, chips)
    swap = pltpu.make_async_remote_copy(
        src_ref=mine, dst_ref=theirs, send_sem=px_send, recv_sem=px_recv,
        device_id=partner, device_id_type=MESH)
    swap.start()

    def send_block(i):
        pltpu.make_async_remote_copy(
            src_ref=in_ref, dst_ref=blocks.at[core, chip], send_sem=in_send, recv_sem=in_recv,
            device_id=device((chip + i) % chips), device_id_type=MESH).start()

    each(1, chips, send_block)
    load(core, 1).wait()
    total = jnp.dot(hidden, w_ref[1], preferred_element_type=F32) - placed(core)
    swap.wait_recv()
    total = (total + theirs[...]).astype(BF16)
    for k in range(pieces):
        q, j = k // cols, k % cols
        part[k] = total[q * tall:(q + 1) * tall, j * LANES:(j + 1) * LANES]

    def send_part(i):
        k = (chip + i) % pieces
        to = (k * stride + shift) % chips

        @pl.when(to != chip)
        def _():
            pltpu.make_async_remote_copy(
                src_ref=part.at[k], dst_ref=landed.at[chip], send_sem=part_send, recv_sem=part_recv,
                device_id=device(to), device_id_type=MESH).start()

    each(0, pieces, send_part)

    @pl.when(owner)
    def _():
        landed[chip] = part[own]
        wait_bytes(landed.at[pl.ds(0, chips - 1)], part_recv)
        reduced = jnp.sum(landed[...].astype(F32), axis=0)
        at = pl.ds(pl.multiple_of(core * half + (own % cols) * LANES, LANES), LANES)
        res[core, own] = (reduced + bias_ref[:, at]).astype(BF16)

        def send_res(i):
            pltpu.make_async_remote_copy(
                src_ref=res.at[core, own], dst_ref=res.at[core, own], send_sem=res_send,
                recv_sem=res_recv, device_id=device((chip + i) % chips),
                device_id_type=MESH).start()

        each(1, chips, send_res)

    wait_bytes(blocks.at[core, pl.ds(0, chips - 1)], in_recv)
    forward = pltpu.make_async_remote_copy(
        src_ref=blocks.at[core], dst_ref=blocks.at[core], send_sem=inx_send, recv_sem=inx_recv,
        device_id=partner, device_id_type=MESH)
    forward.start()
    hid_ref[...] = hidden.astype(F32).T.astype(BF16)
    forward.wait_recv()
    for a in range(narrow):
        for b in range(wide):
            whole[b * block_rows:(b + 1) * block_rows, a * block_cols:(a + 1) * block_cols] = (
                blocks[a % 2, (a // 2) * wide + b].astype(F32))
    cent_ref[...] = (whole[...] - bias_ref[...]).T.astype(BF16)

    @pl.when(owner)
    def _():
        wait_bytes(res.at[core, pl.ds(0, pieces - 1)], res_recv)

    @pl.when(jnp.logical_not(owner))
    def _():
        wait_bytes(res.at[core], res_recv)

    last = pltpu.make_async_remote_copy(
        src_ref=res.at[core], dst_ref=res.at[core], send_sem=rx_send, recv_sem=rx_recv,
        device_id=partner, device_id_type=MESH)
    last.start()
    swap.wait_send()
    forward.wait_send()
    wait_bytes(blocks.at[core, pl.ds(0, chips - 1)], in_send)

    @pl.when(owner)
    def _():
        wait_bytes(part.at[pl.ds(0, pieces - 1)], part_send)
        wait_bytes(landed.at[pl.ds(0, chips - 1)], res_send)

    @pl.when(jnp.logical_not(owner))
    def _():
        wait_bytes(part, part_send)

    last.wait()
    for h in range(2):
        for k in range(pieces):
            q, j = k // cols, k % cols
            at = h * half + j * LANES
            resid_ref[q * tall:(q + 1) * tall, at:at + LANES] = res[h, k]


def gradients(pre_ref, hid_ref, resid_ref, cent_ref, w_ref, enc_hbm, dec_hbm, enc, dec, enc_sem, dec_sem):
    width = resid_ref.shape[1]
    cuts = dec_sem.shape[0]
    step = width // cuts
    copies = []
    for i in range(cuts):
        span = slice(i * step, (i + 1) * step)
        dec[:, span] = jnp.dot(
            hid_ref[...], resid_ref[:, span], preferred_element_type=F32).astype(BF16)
        copies.append(pltpu.make_async_copy(dec.at[:, span], dec_hbm.at[:, span], dec_sem.at[i]))
        copies[-1].start()
    backward = lax.dot_general(
        resid_ref[...], w_ref[...], (((1,), (1,)), ((), ())), preferred_element_type=F32)
    masked = jnp.where(pre_ref[...].astype(F32) > 0, backward, 0.0).astype(BF16)
    for i in range(cuts):
        span = slice(i * step, (i + 1) * step)
        enc[span, :] = jnp.dot(
            cent_ref[span, :], masked, preferred_element_type=F32).astype(BF16)
        copies.append(pltpu.make_async_copy(enc.at[span, :], enc_hbm.at[span, :], enc_sem.at[i]))
        copies[-1].start()
    for copy in copies:
        copy.wait()


def shards(narrow, wide, inputs, decoder_bias, preactivations, decoder_weight):
    rows, features = preactivations.shape
    width = decoder_weight.shape[1]
    half, chips = width // 2, (narrow // 2) * wide
    cols = half // LANES
    groups = 1
    while cols * groups * 2 <= chips and rows % (groups * 2 * 16) == 0:
        groups *= 2
    pieces, tall = cols * groups, rows // groups
    vmem, hbm = pl.BlockSpec(memory_space=pltpu.VMEM), pl.BlockSpec(memory_space=pltpu.HBM)
    dma = pltpu.SemaphoreType.DMA
    resid, centered, hidden = pl.pallas_call(
        functools.partial(exchange, narrow, wide, pieces),
        out_shape=(jax.ShapeDtypeStruct((rows, width), BF16),
                   jax.ShapeDtypeStruct((width, rows), BF16),
                   jax.ShapeDtypeStruct((features, rows), BF16)),
        in_specs=[hbm] * 4,
        out_specs=(vmem,) * 3,
        scratch_shapes=[
            pltpu.VMEM((2, features, half), BF16),
            pltpu.VMEM(inputs.shape, BF16),
            pltpu.VMEM((rows, features), BF16),
            pltpu.VMEM((width,), F32),
            pltpu.VMEM((1, width), F32),
            pltpu.VMEM((8, width), F32),
            pltpu.VMEM((2, chips) + inputs.shape, BF16),
            pltpu.VMEM((rows, width), F32),
            pltpu.VMEM((rows, half), F32),
            pltpu.VMEM((rows, half), F32),
            pltpu.VMEM((pieces, tall, LANES), BF16),
            pltpu.VMEM((chips, tall, LANES), BF16),
            pltpu.VMEM((2, pieces, tall, LANES), BF16),
            dma((2,)),
        ] + [dma] * 15,
        compiler_params=pltpu.CompilerParams(
            collective_id=0, has_side_effects=True, vmem_limit_bytes=32 * 2**20),
        name="exchange",
    )(*(pltpu.with_memory_space_constraint(x, pltpu.HBM)
        for x in (inputs, decoder_bias, preactivations, decoder_weight)))
    cuts = 3
    return pl.pallas_call(
        gradients,
        out_shape=(jax.ShapeDtypeStruct((width, features), BF16),
                   jax.ShapeDtypeStruct((features, width), BF16)),
        in_specs=[vmem] * 5,
        out_specs=(hbm, hbm),
        scratch_shapes=[
            pltpu.VMEM((width, features), BF16),
            pltpu.VMEM((features, width), BF16),
            dma((cuts,)), dma((cuts,)),
        ],
        compiler_params=pltpu.CompilerParams(vmem_limit_bytes=32 * 2**20),
        name="gradients",
    )(preactivations, hidden, resid, centered, decoder_weight)


def solution(mesh):
    placed = (P("wide", "narrow"), P(), P(None, ("narrow", "wide")), P(("narrow", "wide"), None))
    return jax.shard_map(
        functools.partial(shards, mesh.shape["narrow"], mesh.shape["wide"]),
        mesh=mesh,
        in_specs=placed,
        out_specs=(P(None, ("narrow", "wide")), P(("narrow", "wide"), None)),
        check_vma=False,
    )
```

```python
import functools

import jax
import jax.numpy as jnp
from jax import lax
from jax.experimental import pallas as pl
from jax.experimental.pallas import tpu as pltpu
from jax.sharding import PartitionSpec as P

MESH = pl.DeviceIdType.MESH
LANES = 128
BF16 = jnp.bfloat16
F32 = jnp.float32


def each(low, high, body):
    if high - low <= 16:
        for i in range(low, high):
            body(i)
    else:
        lax.fori_loop(low, high, lambda i, _: (body(i), 0)[1], 0)


def div(a, b):
    return a // b if isinstance(a, int) else a if b == 1 else lax.div(a, jnp.int32(b))


def rem(a, b):
    return a % b if isinstance(a, int) else lax.rem(a, jnp.int32(b))


def wait_bytes(ref, sem):
    pltpu.make_async_copy(ref, ref, sem).wait()


def exchange(narrow, wide, pieces, in_hbm, bias_hbm, pre_hbm, w_hbm, resid_ref, cent_ref, hid_ref, dec_ref, back_ref,
             w_ref, in_ref, pre_ref, flat, bias_ref, band, blocks, whole, mine, theirs, part, landed, res,
             w_sem, in_sem, pre_sem, bias_sem, in_send, in_recv, inx_send, inx_recv, px_send, px_recv,
             part_send, part_recv, res_send, res_recv, rx_send, rx_recv):
    n, w = lax.axis_index("narrow"), lax.axis_index("wide")
    core, pair = rem(n, 2), div(n, 2)
    other, chip, pairs = 1 - core, pair * wide + w, narrow // 2
    chips = pairs * wide
    rows, width = whole.shape
    half = width // 2
    cols = half // LANES
    tall = part.shape[1]
    block_rows, block_cols = in_ref.shape
    stride = chips // pieces

    def device(c):
        return {"narrow": div(c, wide) * 2 + core, "wide": rem(c, wide)}

    def peers(body):
        if chips <= 16:
            along = [rem(pair + a, pairs) * 2 + core for a in range(pairs)]
            across = [rem(w + b, wide) for b in range(wide)]
            for b in range(wide):
                for a in range(pairs):
                    if a or b:
                        body({"narrow": along[a], "wide": across[b]})
        else:
            each(1, chips, lambda i: body(device(rem(chip + i, chips))))

    partner = {"narrow": pair * 2 + other, "wide": w}
    turn = core * (pairs // 2)
    place = rem(pair + pairs - turn, pairs) * wide + w
    owner = (rem(place, stride) == 0) & (div(place, stride) < pieces)
    own = lax.min(div(place, stride), pieces - 1)

    def assembled(h):
        return jnp.concatenate([jnp.concatenate([
            res[h, q * cols + j] for j in range(cols)], axis=1) for q in range(pieces // cols)], axis=0)

    def columns(h):
        return pl.ds(pl.multiple_of(h * half, LANES), half)

    def load(h, slot):
        return pltpu.make_async_copy(w_hbm.at[:, columns(h)], w_ref.at[slot], w_sem.at[slot])

    small = [pltpu.make_async_copy(in_hbm, in_ref, in_sem),
             pltpu.make_async_copy(pre_hbm, pre_ref, pre_sem),
             pltpu.make_async_copy(bias_hbm, flat, bias_sem)]
    for copy in small:
        copy.start()
    load(other, 0).start()
    load(core, 1).start()

    barrier = pltpu.get_barrier_semaphore()
    pl.semaphore_signal(barrier, inc=1, device_id=partner, device_id_type=MESH)
    peers(lambda to: pl.semaphore_signal(barrier, inc=1, device_id=to, device_id_type=MESH))

    for copy in small:
        copy.wait()
    block = in_ref[...]
    blocks[core, chip] = block
    bias_ref[...] = flat[...].reshape(1, width)
    for a in range(narrow):
        for b in range(8 // block_rows):
            band[b * block_rows:(b + 1) * block_rows, a * block_cols:(a + 1) * block_cols] = block.astype(F32)

    def placed(h):
        repeated = jnp.concatenate([band[:, columns(h)]] * (rows // 8), axis=0)
        row = lax.broadcasted_iota(jnp.int32, (rows, half), 0) - w * block_rows
        col = lax.broadcasted_iota(jnp.int32, (rows, half), 1) + (h * half - n * block_cols)
        inside = (row >= 0) & (row < block_rows) & (col >= 0) & (col < block_cols)
        return jnp.where(inside, repeated, 0.0)

    hidden = jnp.maximum(pre_ref[...], jnp.zeros_like(pre_ref))
    load(other, 0).wait()
    mine[...] = jnp.dot(hidden, w_ref[0], preferred_element_type=F32) - placed(other)
    pl.semaphore_wait(barrier, chips)
    swap = pltpu.make_async_remote_copy(
        src_ref=mine, dst_ref=theirs, send_sem=px_send, recv_sem=px_recv,
        device_id=partner, device_id_type=MESH)
    swap.start()

    def send_block(to):
        pltpu.make_async_remote_copy(
            src_ref=in_ref, dst_ref=blocks.at[core, chip], send_sem=in_send, recv_sem=in_recv,
            device_id=to, device_id_type=MESH).start()

    peers(send_block)
    load(core, 1).wait()
    total = jnp.dot(hidden, w_ref[1], preferred_element_type=F32) - placed(core)
    swap.wait_recv()
    total = (total + theirs[...]).astype(BF16)
    for k in range(pieces):
        q, j = k // cols, k % cols
        part[k] = total[q * tall:(q + 1) * tall, j * LANES:(j + 1) * LANES]

    def send_part(k):
        row, to_wide = rem(div(k * stride, wide) + turn, pairs), rem(k * stride, wide)

        @pl.when(row * wide + to_wide != chip)
        def _():
            pltpu.make_async_remote_copy(
                src_ref=part.at[k], dst_ref=landed.at[chip], send_sem=part_send, recv_sem=part_recv,
                device_id={"narrow": row * 2 + core, "wide": to_wide}, device_id_type=MESH).start()

    each(0, pieces, send_part)

    @pl.when(owner)
    def _():
        landed[chip] = part[own]
        wait_bytes(landed.at[pl.ds(0, chips - 1)], part_recv)
        reduced = jnp.sum(landed[...].astype(F32), axis=0)
        at = pl.ds(pl.multiple_of(core * half + (own % cols) * LANES, LANES), LANES)
        res[core, own] = (reduced + bias_ref[:, at]).astype(BF16)

        def send_res(to):
            pltpu.make_async_remote_copy(
                src_ref=res.at[core, own], dst_ref=res.at[core, own], send_sem=res_send,
                recv_sem=res_recv, device_id=to, device_id_type=MESH).start()

        peers(send_res)

    wait_bytes(blocks.at[core, pl.ds(0, chips - 1)], in_recv)
    forward = pltpu.make_async_remote_copy(
        src_ref=blocks.at[core], dst_ref=blocks.at[core], send_sem=inx_send, recv_sem=inx_recv,
        device_id=partner, device_id_type=MESH)
    forward.start()
    hid_ref[...] = hidden.astype(F32).T.astype(BF16)
    forward.wait_recv()
    for a in range(narrow):
        for b in range(wide):
            whole[b * block_rows:(b + 1) * block_rows, a * block_cols:(a + 1) * block_cols] = (
                blocks[a % 2, (a // 2) * wide + b].astype(F32))
    cent_ref[...] = (whole[...] - bias_ref[...]).T.astype(BF16)

    @pl.when(owner)
    def _():
        wait_bytes(res.at[core, pl.ds(0, pieces - 1)], res_recv)

    @pl.when(jnp.logical_not(owner))
    def _():
        wait_bytes(res.at[core], res_recv)

    last = pltpu.make_async_remote_copy(
        src_ref=res.at[core], dst_ref=res.at[core], send_sem=rx_send, recv_sem=rx_recv,
        device_id=partner, device_id_type=MESH)
    last.start()
    first = assembled(core)
    dec_ref[...] = jnp.dot(hid_ref[...], first, preferred_element_type=F32).astype(BF16)
    back_ref[...] = lax.dot_general(first, w_ref[1], (((1,), (1,)), ((), ())), preferred_element_type=F32)
    swap.wait_send()
    forward.wait_send()
    wait_bytes(blocks.at[core, pl.ds(0, chips - 1)], in_send)

    @pl.when(owner)
    def _():
        wait_bytes(part.at[pl.ds(0, pieces - 1)], part_send)
        wait_bytes(landed.at[pl.ds(0, chips - 1)], res_send)

    @pl.when(jnp.logical_not(owner))
    def _():
        wait_bytes(part, part_send)

    last.wait()
    resid_ref[...] = assembled(other)


def gradients(hid_ref, resid_ref, cent_ref, dec_ref, back_ref, pre_ref, w_ref, enc_hbm, dec_hbm,
              enc, dec, enc_sem, dec_sem):
    core = rem(lax.axis_index("narrow"), 2)
    half = resid_ref.shape[1]

    def columns(h):
        return pl.ds(pl.multiple_of(h * half, LANES), half)

    copies = [pltpu.make_async_copy(dec_ref, dec_hbm.at[:, columns(core)], dec_sem.at[0])]
    copies[0].start()
    backward = back_ref[...] + lax.dot_general(
        resid_ref[...], w_ref[:, columns(1 - core)], (((1,), (1,)), ((), ())), preferred_element_type=F32)
    masked = jnp.where(pre_ref[...].astype(F32) > 0, backward, 0.0).astype(BF16)
    dec[...] = jnp.dot(hid_ref[...], resid_ref[...], preferred_element_type=F32).astype(BF16)
    copies.append(pltpu.make_async_copy(dec, dec_hbm.at[:, columns(1 - core)], dec_sem.at[1]))
    copies[1].start()
    cuts = enc_sem.shape[0]
    step = enc.shape[0] // cuts
    for i in range(cuts):
        span = slice(i * step, (i + 1) * step)
        enc[span, :] = jnp.dot(
            cent_ref[span, :], masked, preferred_element_type=F32).astype(BF16)
        copies.append(pltpu.make_async_copy(enc.at[span, :], enc_hbm.at[span, :], enc_sem.at[i]))
        copies[-1].start()
    for copy in copies:
        copy.wait()


def shards(narrow, wide, inputs, decoder_bias, preactivations, decoder_weight):
    rows, features = preactivations.shape
    width = decoder_weight.shape[1]
    half, chips = width // 2, (narrow // 2) * wide
    cols = half // LANES
    groups = 1
    while cols * groups * 2 <= chips and rows % (groups * 2 * 16) == 0:
        groups *= 2
    pieces, tall = cols * groups, rows // groups
    vmem, hbm = pl.BlockSpec(memory_space=pltpu.VMEM), pl.BlockSpec(memory_space=pltpu.HBM)
    dma = pltpu.SemaphoreType.DMA
    kept = pl.pallas_call(
        functools.partial(exchange, narrow, wide, pieces),
        out_shape=(jax.ShapeDtypeStruct((rows, half), BF16),
                   jax.ShapeDtypeStruct((width, rows), BF16),
                   jax.ShapeDtypeStruct((features, rows), BF16),
                   jax.ShapeDtypeStruct((features, half), BF16),
                   jax.ShapeDtypeStruct((rows, features), F32)),
        in_specs=[hbm] * 4,
        out_specs=(vmem,) * 5,
        scratch_shapes=[
            pltpu.VMEM((2, features, half), BF16),
            pltpu.VMEM(inputs.shape, BF16),
            pltpu.VMEM((rows, features), BF16),
            pltpu.VMEM((width,), F32),
            pltpu.VMEM((1, width), F32),
            pltpu.VMEM((8, width), F32),
            pltpu.VMEM((2, chips) + inputs.shape, BF16),
            pltpu.VMEM((rows, width), F32),
            pltpu.VMEM((rows, half), F32),
            pltpu.VMEM((rows, half), F32),
            pltpu.VMEM((pieces, tall, LANES), BF16),
            pltpu.VMEM((chips, tall, LANES), BF16),
            pltpu.VMEM((2, pieces, tall, LANES), BF16),
            dma((2,)),
        ] + [dma] * 15,
        compiler_params=pltpu.CompilerParams(
            collective_id=0, has_side_effects=True, vmem_limit_bytes=32 * 2**20),
        name="exchange",
    )(*(pltpu.with_memory_space_constraint(x, pltpu.HBM)
        for x in (inputs, decoder_bias, preactivations, decoder_weight)))
    resid, centered, hidden, decoder, backward = kept
    return pl.pallas_call(
        gradients,
        out_shape=(jax.ShapeDtypeStruct((width, features), BF16),
                   jax.ShapeDtypeStruct((features, width), BF16)),
        in_specs=[vmem] * 7,
        out_specs=(hbm, hbm),
        scratch_shapes=[
            pltpu.VMEM((width, features), BF16),
            pltpu.VMEM((features, half), BF16),
            dma((3,)), dma((2,)),
        ],
        compiler_params=pltpu.CompilerParams(vmem_limit_bytes=32 * 2**20),
        name="gradients",
    )(hidden, resid, centered, decoder, backward, preactivations, decoder_weight)


def solution(mesh):
    placed = (P("wide", "narrow"), P(), P(None, ("narrow", "wide")), P(("narrow", "wide"), None))
    return jax.shard_map(
        functools.partial(shards, mesh.shape["narrow"], mesh.shape["wide"]),
        mesh=mesh,
        in_specs=placed,
        out_specs=(P(None, ("narrow", "wide")), P(("narrow", "wide"), None)),
        check_vma=False,
    )
```

```python
import functools

import jax
import jax.numpy as jnp
from jax import lax
from jax.experimental import pallas as pl
from jax.experimental.pallas import tpu as pltpu
from jax.sharding import PartitionSpec as P

MESH = pl.DeviceIdType.MESH
LANES = 128
BF16 = jnp.bfloat16
F32 = jnp.float32


def each(low, high, body):
    if high - low <= 16:
        for i in range(low, high):
            body(i)
    else:
        lax.fori_loop(low, high, lambda i, _: (body(i), 0)[1], 0)


def div(a, b):
    return a // b if isinstance(a, int) else a if b == 1 else lax.div(a, jnp.int32(b))


def rem(a, b):
    return a % b if isinstance(a, int) else lax.rem(a, jnp.int32(b))


def wait_bytes(ref, sem):
    pltpu.make_async_copy(ref, ref, sem).wait()


def exchange(narrow, wide, pieces, in_hbm, bias_hbm, pre_hbm, w_hbm, resid_ref, cent_ref, hid_ref, dec_ref, back_ref,
             w_ref, in_ref, pre_ref, flat, bias_ref, band, blocks, whole, mine, theirs, part, landed, res,
             w_sem, in_sem, pre_sem, bias_sem, in_send, in_recv, inx_send, inx_recv, px_send, px_recv,
             part_send, part_recv, res_send, res_recv, rx_send, rx_recv):
    n, w = lax.axis_index("narrow"), lax.axis_index("wide")
    core, pair = rem(n, 2), div(n, 2)
    other, chip, pairs = 1 - core, pair * wide + w, narrow // 2
    chips = pairs * wide
    rows, width = whole.shape
    half = width // 2
    cols = half // LANES
    tall = part.shape[1]
    block_rows, block_cols = in_ref.shape
    stride = chips // pieces

    def device(c):
        return {"narrow": div(c, wide) * 2 + core, "wide": rem(c, wide)}

    def peers(body):
        if chips <= 16:
            along = [rem(pair + a, pairs) * 2 + core for a in range(pairs)]
            across = [rem(w + b, wide) for b in range(wide)]
            for b in range(wide):
                for a in range(pairs):
                    if a or b:
                        body({"narrow": along[a], "wide": across[b]})
        else:
            each(1, chips, lambda i: body(device(rem(chip + i, chips))))

    partner = {"narrow": pair * 2 + other, "wide": w}
    turn = core * (pairs // 2)
    place = rem(pair + pairs - turn, pairs) * wide + w
    owner = (rem(place, stride) == 0) & (div(place, stride) < pieces)
    own = lax.min(div(place, stride), pieces - 1)

    def assembled(h):
        return jnp.concatenate([jnp.concatenate([
            res[h, q * cols + j] for j in range(cols)], axis=1) for q in range(pieces // cols)], axis=0)

    def columns(h):
        return pl.ds(pl.multiple_of(h * half, LANES), half)

    def load(h, slot):
        return pltpu.make_async_copy(w_hbm.at[:, columns(h)], w_ref.at[slot], w_sem.at[slot])

    small = [pltpu.make_async_copy(in_hbm, in_ref, in_sem),
             pltpu.make_async_copy(pre_hbm, pre_ref, pre_sem),
             pltpu.make_async_copy(bias_hbm, flat, bias_sem)]
    for copy in small:
        copy.start()
    load(other, 0).start()
    load(core, 1).start()

    barrier = pltpu.get_barrier_semaphore()
    for a in range(pairs):
        pl.semaphore_signal(barrier, inc=1, device_id_type=MESH, device_id={
            "narrow": rem(pair + a, pairs) * 2 + other, "wide": w})
    peers(lambda to: pl.semaphore_signal(barrier, inc=1, device_id=to, device_id_type=MESH))

    for copy in small:
        copy.wait()
    block = in_ref[...]
    blocks[n, w] = block
    bias_ref[...] = flat[...].reshape(1, width)
    for a in range(narrow):
        for b in range(8 // block_rows):
            band[b * block_rows:(b + 1) * block_rows, a * block_cols:(a + 1) * block_cols] = block.astype(F32)

    def placed(h):
        repeated = jnp.concatenate([band[:, columns(h)]] * (rows // 8), axis=0)
        row = lax.broadcasted_iota(jnp.int32, (rows, half), 0) - w * block_rows
        col = lax.broadcasted_iota(jnp.int32, (rows, half), 1) + (h * half - n * block_cols)
        inside = (row >= 0) & (row < block_rows) & (col >= 0) & (col < block_cols)
        return jnp.where(inside, repeated, 0.0)

    hidden = jnp.maximum(pre_ref[...], jnp.zeros_like(pre_ref))
    load(other, 0).wait()
    mine[...] = jnp.dot(hidden, w_ref[0], preferred_element_type=F32) - placed(other)
    pl.semaphore_wait(barrier, chips - 1 + pairs)
    swap = pltpu.make_async_remote_copy(
        src_ref=mine, dst_ref=theirs, send_sem=px_send, recv_sem=px_recv,
        device_id=partner, device_id_type=MESH)
    swap.start()

    def send_block(b):
        pltpu.make_async_remote_copy(
            src_ref=in_ref, dst_ref=blocks.at[n, w], send_sem=in_send, recv_sem=in_recv,
            device_id={"narrow": n, "wide": rem(w + b, wide)}, device_id_type=MESH).start()

    each(1, wide, send_block)
    load(core, 1).wait()
    total = jnp.dot(hidden, w_ref[1], preferred_element_type=F32) - placed(core)
    swap.wait_recv()
    total = (total + theirs[...]).astype(BF16)
    for k in range(pieces):
        q, j = k // cols, k % cols
        part[k] = total[q * tall:(q + 1) * tall, j * LANES:(j + 1) * LANES]

    def send_part(k):
        row, to_wide = rem(div(k * stride, wide) + turn, pairs), rem(k * stride, wide)

        @pl.when(row * wide + to_wide != chip)
        def _():
            pltpu.make_async_remote_copy(
                src_ref=part.at[k], dst_ref=landed.at[chip], send_sem=part_send, recv_sem=part_recv,
                device_id={"narrow": row * 2 + core, "wide": to_wide}, device_id_type=MESH).start()

    each(0, pieces, send_part)
    wait_bytes(blocks.at[n, pl.ds(0, wide - 1)], in_recv)

    def send_blocks(a):
        pltpu.make_async_remote_copy(
            src_ref=blocks.at[n], dst_ref=blocks.at[n], send_sem=inx_send, recv_sem=inx_recv,
            device_id={"narrow": rem(n + a, narrow), "wide": w}, device_id_type=MESH).start()

    each(1, narrow, send_blocks)
    hid_ref[...] = hidden.astype(F32).T.astype(BF16)

    @pl.when(owner)
    def _():
        landed[chip] = part[own]
        wait_bytes(landed.at[pl.ds(0, chips - 1)], part_recv)
        reduced = jnp.sum(landed[...].astype(F32), axis=0)
        at = pl.ds(pl.multiple_of(core * half + (own % cols) * LANES, LANES), LANES)
        res[core, own] = (reduced + bias_ref[:, at]).astype(BF16)

        def send_res(to):
            pltpu.make_async_remote_copy(
                src_ref=res.at[core, own], dst_ref=res.at[core, own], send_sem=res_send,
                recv_sem=res_recv, device_id=to, device_id_type=MESH).start()

        peers(send_res)

    wait_bytes(blocks.at[pl.ds(0, narrow - 1)], inx_recv)
    for a in range(narrow):
        for b in range(wide):
            whole[b * block_rows:(b + 1) * block_rows, a * block_cols:(a + 1) * block_cols] = (
                blocks[a, b].astype(F32))
    cent_ref[...] = (whole[...] - bias_ref[...]).T.astype(BF16)

    @pl.when(owner)
    def _():
        wait_bytes(res.at[core, pl.ds(0, pieces - 1)], res_recv)

    @pl.when(jnp.logical_not(owner))
    def _():
        wait_bytes(res.at[core], res_recv)

    last = pltpu.make_async_remote_copy(
        src_ref=res.at[core], dst_ref=res.at[core], send_sem=rx_send, recv_sem=rx_recv,
        device_id=partner, device_id_type=MESH)
    last.start()
    first = assembled(core)
    dec_ref[...] = jnp.dot(hid_ref[...], first, preferred_element_type=F32).astype(BF16)
    back_ref[...] = lax.dot_general(first, w_ref[1], (((1,), (1,)), ((), ())), preferred_element_type=F32)
    swap.wait_send()
    wait_bytes(blocks.at[n, pl.ds(0, wide - 1)], in_send)
    wait_bytes(blocks.at[pl.ds(0, narrow - 1)], inx_send)

    @pl.when(owner)
    def _():
        wait_bytes(part.at[pl.ds(0, pieces - 1)], part_send)
        wait_bytes(landed.at[pl.ds(0, chips - 1)], res_send)

    @pl.when(jnp.logical_not(owner))
    def _():
        wait_bytes(part, part_send)

    last.wait()
    resid_ref[...] = assembled(other)


def gradients(hid_ref, resid_ref, cent_ref, dec_ref, back_ref, pre_ref, w_ref, enc_hbm, dec_hbm,
              enc, dec, enc_sem, dec_sem):
    core = rem(lax.axis_index("narrow"), 2)
    half = resid_ref.shape[1]

    def columns(h):
        return pl.ds(pl.multiple_of(h * half, LANES), half)

    copies = [pltpu.make_async_copy(dec_ref, dec_hbm.at[:, columns(core)], dec_sem.at[0])]
    copies[0].start()
    backward = back_ref[...] + lax.dot_general(
        resid_ref[...], w_ref[:, columns(1 - core)], (((1,), (1,)), ((), ())), preferred_element_type=F32)
    masked = jnp.where(pre_ref[...].astype(F32) > 0, backward, 0.0).astype(BF16)
    dec[...] = jnp.dot(hid_ref[...], resid_ref[...], preferred_element_type=F32).astype(BF16)
    copies.append(pltpu.make_async_copy(dec, dec_hbm.at[:, columns(1 - core)], dec_sem.at[1]))
    copies[1].start()
    cuts = enc_sem.shape[0]
    step = enc.shape[0] // cuts
    for i in range(cuts):
        span = slice(i * step, (i + 1) * step)
        enc[span, :] = jnp.dot(
            cent_ref[span, :], masked, preferred_element_type=F32).astype(BF16)
        copies.append(pltpu.make_async_copy(enc.at[span, :], enc_hbm.at[span, :], enc_sem.at[i]))
        copies[-1].start()
    for copy in copies:
        copy.wait()


def shards(narrow, wide, inputs, decoder_bias, preactivations, decoder_weight):
    rows, features = preactivations.shape
    width = decoder_weight.shape[1]
    half, chips = width // 2, (narrow // 2) * wide
    cols = half // LANES
    groups = 1
    while cols * groups * 2 <= chips and rows % (groups * 2 * 16) == 0:
        groups *= 2
    pieces, tall = cols * groups, rows // groups
    vmem, hbm = pl.BlockSpec(memory_space=pltpu.VMEM), pl.BlockSpec(memory_space=pltpu.HBM)
    dma = pltpu.SemaphoreType.DMA
    kept = pl.pallas_call(
        functools.partial(exchange, narrow, wide, pieces),
        out_shape=(jax.ShapeDtypeStruct((rows, half), BF16),
                   jax.ShapeDtypeStruct((width, rows), BF16),
                   jax.ShapeDtypeStruct((features, rows), BF16),
                   jax.ShapeDtypeStruct((features, half), BF16),
                   jax.ShapeDtypeStruct((rows, features), F32)),
        in_specs=[hbm] * 4,
        out_specs=(vmem,) * 5,
        scratch_shapes=[
            pltpu.VMEM((2, features, half), BF16),
            pltpu.VMEM(inputs.shape, BF16),
            pltpu.VMEM((rows, features), BF16),
            pltpu.VMEM((width,), F32),
            pltpu.VMEM((1, width), F32),
            pltpu.VMEM((8, width), F32),
            pltpu.VMEM((narrow, wide) + inputs.shape, BF16),
            pltpu.VMEM((rows, width), F32),
            pltpu.VMEM((rows, half), F32),
            pltpu.VMEM((rows, half), F32),
            pltpu.VMEM((pieces, tall, LANES), BF16),
            pltpu.VMEM((chips, tall, LANES), BF16),
            pltpu.VMEM((2, pieces, tall, LANES), BF16),
            dma((2,)),
        ] + [dma] * 15,
        compiler_params=pltpu.CompilerParams(
            collective_id=0, has_side_effects=True, vmem_limit_bytes=32 * 2**20),
        name="exchange",
    )(*(pltpu.with_memory_space_constraint(x, pltpu.HBM)
        for x in (inputs, decoder_bias, preactivations, decoder_weight)))
    resid, centered, hidden, decoder, backward = kept
    return pl.pallas_call(
        gradients,
        out_shape=(jax.ShapeDtypeStruct((width, features), BF16),
                   jax.ShapeDtypeStruct((features, width), BF16)),
        in_specs=[vmem] * 7,
        out_specs=(hbm, hbm),
        scratch_shapes=[
            pltpu.VMEM((width, features), BF16),
            pltpu.VMEM((features, half), BF16),
            dma((3,)), dma((2,)),
        ],
        compiler_params=pltpu.CompilerParams(vmem_limit_bytes=32 * 2**20),
        name="gradients",
    )(hidden, resid, centered, decoder, backward, preactivations, decoder_weight)


def solution(mesh):
    placed = (P("wide", "narrow"), P(), P(None, ("narrow", "wide")), P(("narrow", "wide"), None))
    return jax.shard_map(
        functools.partial(shards, mesh.shape["narrow"], mesh.shape["wide"]),
        mesh=mesh,
        in_specs=placed,
        out_specs=(P(None, ("narrow", "wide")), P(("narrow", "wide"), None)),
        check_vma=False,
    )
```

```python
import functools

import jax
import jax.numpy as jnp
from jax import lax
from jax.experimental import pallas as pl
from jax.experimental.pallas import tpu as pltpu
from jax.sharding import PartitionSpec as P

MESH = pl.DeviceIdType.MESH
LANES = 128
BF16 = jnp.bfloat16
F32 = jnp.float32


def each(low, high, body):
    if high - low <= 16:
        for i in range(low, high):
            body(i)
    else:
        lax.fori_loop(low, high, lambda i, _: (body(i), 0)[1], 0)


def div(a, b):
    return a // b if isinstance(a, int) else a if b == 1 else lax.div(a, jnp.int32(b))


def rem(a, b):
    return a % b if isinstance(a, int) else lax.rem(a, jnp.int32(b))


def wait_bytes(ref, sem):
    pltpu.make_async_copy(ref, ref, sem).wait()


def exchange(narrow, wide, pieces, in_hbm, bias_hbm, pre_hbm, w_hbm, resid_ref, cent_ref, hid_ref, dec_ref, back_ref,
             w_ref, in_ref, pre_ref, flat, bias_ref, band, blocks, whole, mine, kept, theirs, part, landed, res,
             w_sem, in_sem, pre_sem, bias_sem, in_send, in_recv, inx_send, inx_recv, px_send, px_recv,
             part_send, part_recv, res_send, res_recv, rx_send, rx_recv):
    n, w = lax.axis_index("narrow"), lax.axis_index("wide")
    core, pair = rem(n, 2), div(n, 2)
    other, chip, pairs = 1 - core, pair * wide + w, narrow // 2
    chips = pairs * wide
    rows, width = whole.shape
    half = width // 2
    cols = half // LANES
    tall = part.shape[1]
    block_rows, block_cols = in_ref.shape
    depth, edge = wide // 2, wide // 4
    owners = pairs * depth
    rounds = -(-pieces // owners)

    def peers(body):
        if chips <= 16:
            along = [rem(pair + a, pairs) * 2 + core for a in range(pairs)]
            across = [rem(w + b, wide) for b in range(wide)]
            for b in range(wide):
                for a in range(pairs):
                    if a or b:
                        body({"narrow": along[a], "wide": across[b]}, a, b)
        else:
            def one(i):
                a, b = div(i, wide), rem(i, wide)
                body({"narrow": rem(pair + a, pairs) * 2 + core, "wide": rem(w + b, wide)}, a, b)
            each(1, chips, one)

    partner = {"narrow": pair * 2 + other, "wide": w}
    turn = core * (pairs // 2)
    middle = (w >= edge) & (w < edge + depth)
    seat = rem(pair + pairs - turn, pairs) * depth + lax.min(lax.max(w - edge, 0), depth - 1)
    held = [middle & (seat + r * owners < pieces) for r in range(rounds)]
    owned = [lax.min(seat + r * owners, pieces - 1) for r in range(rounds)]

    def by_count(body):
        for count in range(rounds + 1):
            at_least = held[count - 1] if count else None
            below = jnp.logical_not(held[count]) if count < rounds else None
            both = below if at_least is None else at_least if below is None else at_least & below
            pl.when(both)(functools.partial(body, count))

    def assembled(h):
        return jnp.concatenate([jnp.concatenate([
            res[h, q * cols + j] for j in range(cols)], axis=1) for q in range(pieces // cols)], axis=0)

    def columns(h):
        return pl.ds(pl.multiple_of(h * half, LANES), half)

    def load(h, slot):
        return pltpu.make_async_copy(w_hbm.at[:, columns(h)], w_ref.at[slot], w_sem.at[slot])

    small = [pltpu.make_async_copy(in_hbm, in_ref, in_sem),
             pltpu.make_async_copy(pre_hbm, pre_ref, pre_sem),
             pltpu.make_async_copy(bias_hbm, flat, bias_sem)]
    for copy in small:
        copy.start()
    load(other, 0).start()
    load(core, 1).start()

    barrier = pltpu.get_barrier_semaphore()
    for a in range(pairs):
        pl.semaphore_signal(barrier, inc=1, device_id_type=MESH, device_id={
            "narrow": rem(pair + a, pairs) * 2 + other, "wide": w})

    def greet(to, a, b):
        def signal():
            pl.semaphore_signal(barrier, inc=1, device_id=to, device_id_type=MESH)

        if isinstance(a, int) and (a == 0 or b == 0):
            signal()
        else:
            there = (to["wide"] >= edge) & (to["wide"] < edge + depth)
            pl.when(middle | there | (a == 0) | (b == 0))(signal)

    peers(greet)

    for copy in small:
        copy.wait()
    block = in_ref[...]
    blocks[n, w] = block
    bias_ref[...] = flat[...].reshape(1, width)
    for a in range(narrow):
        for b in range(8 // block_rows):
            band[b * block_rows:(b + 1) * block_rows, a * block_cols:(a + 1) * block_cols] = block.astype(F32)

    def placed(h):
        repeated = jnp.concatenate([band[:, columns(h)]] * (rows // 8), axis=0)
        row = lax.broadcasted_iota(jnp.int32, (rows, half), 0) - w * block_rows
        col = lax.broadcasted_iota(jnp.int32, (rows, half), 1) + (h * half - n * block_cols)
        inside = (row >= 0) & (row < block_rows) & (col >= 0) & (col < block_cols)
        return jnp.where(inside, repeated, 0.0)

    hidden = jnp.maximum(pre_ref[...], jnp.zeros_like(pre_ref))
    load(other, 0).wait()
    mine[...] = jnp.dot(hidden, w_ref[0], preferred_element_type=F32) - placed(other)
    load(core, 1).wait()
    kept[...] = jnp.dot(hidden, w_ref[1], preferred_element_type=F32) - placed(core)

    @pl.when(middle)
    def _():
        pl.semaphore_wait(barrier, pairs + chips - 1)

    @pl.when(jnp.logical_not(middle))
    def _():
        pl.semaphore_wait(barrier, pairs + owners + wide - depth - 1 + pairs - 1)

    swap = pltpu.make_async_remote_copy(
        src_ref=mine, dst_ref=theirs, send_sem=px_send, recv_sem=px_recv,
        device_id=partner, device_id_type=MESH)
    swap.start()

    def send_block(b):
        pltpu.make_async_remote_copy(
            src_ref=in_ref, dst_ref=blocks.at[n, w], send_sem=in_send, recv_sem=in_recv,
            device_id={"narrow": n, "wide": rem(w + b, wide)}, device_id_type=MESH).start()

    each(1, wide, send_block)
    swap.wait_recv()
    total = (kept[...] + theirs[...]).astype(BF16)
    for k in range(pieces):
        q, j = k // cols, k % cols
        part[k] = total[q * tall:(q + 1) * tall, j * LANES:(j + 1) * LANES]

    def send_part(k):
        spot, r = rem(k, owners), div(k, owners)
        row, to_wide = rem(div(spot, depth) + turn, pairs), edge + rem(spot, depth)

        @pl.when(row * wide + to_wide != chip)
        def _():
            pltpu.make_async_remote_copy(
                src_ref=part.at[k], dst_ref=landed.at[r, chip], send_sem=part_send, recv_sem=part_recv.at[r],
                device_id={"narrow": row * 2 + core, "wide": to_wide}, device_id_type=MESH).start()

    each(0, pieces, send_part)
    wait_bytes(blocks.at[n, pl.ds(0, wide - 1)], in_recv)

    def send_blocks(a):
        pltpu.make_async_remote_copy(
            src_ref=blocks.at[n], dst_ref=blocks.at[n], send_sem=inx_send, recv_sem=inx_recv,
            device_id={"narrow": rem(n + a, narrow), "wide": w}, device_id_type=MESH).start()

    each(1, narrow, send_blocks)
    hid_ref[...] = hidden.astype(F32).T.astype(BF16)

    def finish(r):
        own = owned[r]
        landed[r, chip] = part[own]
        wait_bytes(landed.at[r, pl.ds(0, chips - 1)], part_recv.at[r])
        reduced = jnp.sum(landed[r].astype(F32), axis=0)
        at = pl.ds(pl.multiple_of(core * half + rem(own, cols) * LANES, LANES), LANES)
        res[core, own] = (reduced + bias_ref[:, at]).astype(BF16)

        def send_res(to, a, b):
            pltpu.make_async_remote_copy(
                src_ref=res.at[core, own], dst_ref=res.at[core, own], send_sem=res_send.at[r],
                recv_sem=res_recv, device_id=to, device_id_type=MESH).start()

        peers(send_res)

    for r in range(rounds):
        pl.when(held[r])(functools.partial(finish, r))

    wait_bytes(blocks.at[pl.ds(0, narrow - 1)], inx_recv)
    for a in range(narrow):
        for b in range(wide):
            whole[b * block_rows:(b + 1) * block_rows, a * block_cols:(a + 1) * block_cols] = (
                blocks[a, b].astype(F32))
    cent_ref[...] = (whole[...] - bias_ref[...]).T.astype(BF16)

    by_count(lambda count: wait_bytes(res.at[core, pl.ds(0, pieces - count)], res_recv))
    last = pltpu.make_async_remote_copy(
        src_ref=res.at[core], dst_ref=res.at[core], send_sem=rx_send, recv_sem=rx_recv,
        device_id=partner, device_id_type=MESH)
    last.start()
    first = assembled(core)
    dec_ref[...] = jnp.dot(hid_ref[...], first, preferred_element_type=F32).astype(BF16)
    back_ref[...] = lax.dot_general(first, w_ref[1], (((1,), (1,)), ((), ())), preferred_element_type=F32)
    swap.wait_send()
    wait_bytes(blocks.at[n, pl.ds(0, wide - 1)], in_send)
    wait_bytes(blocks.at[pl.ds(0, narrow - 1)], inx_send)

    by_count(lambda count: wait_bytes(part.at[pl.ds(0, pieces - count)], part_send))
    for r in range(rounds):
        pl.when(held[r])(functools.partial(
            wait_bytes, landed.at[r, pl.ds(0, chips - 1)], res_send.at[r]))
    last.wait()
    resid_ref[...] = assembled(other)


def gradients(hid_ref, resid_ref, cent_ref, dec_ref, back_ref, pre_ref, w_ref, enc_hbm, dec_hbm,
              enc, dec, enc_sem, dec_sem):
    core = rem(lax.axis_index("narrow"), 2)
    half = resid_ref.shape[1]

    def columns(h):
        return pl.ds(pl.multiple_of(h * half, LANES), half)

    copies = [pltpu.make_async_copy(dec_ref, dec_hbm.at[:, columns(core)], dec_sem.at[0])]
    copies[0].start()
    backward = back_ref[...] + lax.dot_general(
        resid_ref[...], w_ref[:, columns(1 - core)], (((1,), (1,)), ((), ())), preferred_element_type=F32)
    masked = jnp.where(pre_ref[...].astype(F32) > 0, backward, 0.0).astype(BF16)
    dec[...] = jnp.dot(hid_ref[...], resid_ref[...], preferred_element_type=F32).astype(BF16)
    copies.append(pltpu.make_async_copy(dec, dec_hbm.at[:, columns(1 - core)], dec_sem.at[1]))
    copies[1].start()
    cuts = enc_sem.shape[0]
    step = enc.shape[0] // cuts
    for i in range(cuts):
        span = slice(i * step, (i + 1) * step)
        enc[span, :] = jnp.dot(
            cent_ref[span, :], masked, preferred_element_type=F32).astype(BF16)
        copies.append(pltpu.make_async_copy(enc.at[span, :], enc_hbm.at[span, :], enc_sem.at[i]))
        copies[-1].start()
    for copy in copies:
        copy.wait()


def shards(narrow, wide, inputs, decoder_bias, preactivations, decoder_weight):
    rows, features = preactivations.shape
    width = decoder_weight.shape[1]
    half, chips = width // 2, (narrow // 2) * wide
    cols = half // LANES
    groups = 1
    while cols * groups * 2 <= chips and rows % (groups * 2 * 16) == 0:
        groups *= 2
    pieces, tall = cols * groups, rows // groups
    rounds = -(-pieces // (narrow // 2 * (wide // 2)))
    vmem, hbm = pl.BlockSpec(memory_space=pltpu.VMEM), pl.BlockSpec(memory_space=pltpu.HBM)
    dma = pltpu.SemaphoreType.DMA
    kept = pl.pallas_call(
        functools.partial(exchange, narrow, wide, pieces),
        out_shape=(jax.ShapeDtypeStruct((rows, half), BF16),
                   jax.ShapeDtypeStruct((width, rows), BF16),
                   jax.ShapeDtypeStruct((features, rows), BF16),
                   jax.ShapeDtypeStruct((features, half), BF16),
                   jax.ShapeDtypeStruct((rows, features), F32)),
        in_specs=[hbm] * 4,
        out_specs=(vmem,) * 5,
        scratch_shapes=[
            pltpu.VMEM((2, features, half), BF16),
            pltpu.VMEM(inputs.shape, BF16),
            pltpu.VMEM((rows, features), BF16),
            pltpu.VMEM((width,), F32),
            pltpu.VMEM((1, width), F32),
            pltpu.VMEM((8, width), F32),
            pltpu.VMEM((narrow, wide) + inputs.shape, BF16),
            pltpu.VMEM((rows, width), F32),
            pltpu.VMEM((rows, half), F32),
            pltpu.VMEM((rows, half), F32),
            pltpu.VMEM((rows, half), F32),
            pltpu.VMEM((pieces, tall, LANES), BF16),
            pltpu.VMEM((rounds, chips, tall, LANES), BF16),
            pltpu.VMEM((2, pieces, tall, LANES), BF16),
            dma((2,)),
        ] + [dma] * 10 + [dma((rounds,)), dma((rounds,)), dma, dma, dma],
        compiler_params=pltpu.CompilerParams(
            collective_id=0, has_side_effects=True, vmem_limit_bytes=32 * 2**20),
        name="exchange",
    )(*(pltpu.with_memory_space_constraint(x, pltpu.HBM)
        for x in (inputs, decoder_bias, preactivations, decoder_weight)))
    resid, centered, hidden, decoder, backward = kept
    return pl.pallas_call(
        gradients,
        out_shape=(jax.ShapeDtypeStruct((width, features), BF16),
                   jax.ShapeDtypeStruct((features, width), BF16)),
        in_specs=[vmem] * 7,
        out_specs=(hbm, hbm),
        scratch_shapes=[
            pltpu.VMEM((width, features), BF16),
            pltpu.VMEM((features, half), BF16),
            dma((3,)), dma((2,)),
        ],
        compiler_params=pltpu.CompilerParams(vmem_limit_bytes=32 * 2**20),
        name="gradients",
    )(hidden, resid, centered, decoder, backward, preactivations, decoder_weight)


def solution(mesh):
    placed = (P("wide", "narrow"), P(), P(None, ("narrow", "wide")), P(("narrow", "wide"), None))
    return jax.shard_map(
        functools.partial(shards, mesh.shape["narrow"], mesh.shape["wide"]),
        mesh=mesh,
        in_specs=placed,
        out_specs=(P(None, ("narrow", "wide")), P(("narrow", "wide"), None)),
        check_vma=False,
    )
```

```python
import functools

import jax
import jax.numpy as jnp
from jax import lax
from jax.experimental import pallas as pl
from jax.experimental.pallas import tpu as pltpu
from jax.sharding import PartitionSpec as P

MESH = pl.DeviceIdType.MESH
LANES = 128
BF16 = jnp.bfloat16
F32 = jnp.float32


def each(low, high, body):
    if high - low <= 16:
        for i in range(low, high):
            body(i)
    else:
        lax.fori_loop(low, high, lambda i, _: (body(i), 0)[1], 0)


def div(a, b):
    return a // b if isinstance(a, int) else a if b == 1 else lax.div(a, jnp.int32(b))


def rem(a, b):
    return a % b if isinstance(a, int) else lax.rem(a, jnp.int32(b))


def wait_bytes(ref, sem):
    pltpu.make_async_copy(ref, ref, sem).wait()


def exchange(narrow, wide, pieces, in_hbm, bias_hbm, pre_hbm, w_hbm, resid_ref, cent_ref, hid_ref, dec_ref, back_ref,
             w_ref, in_ref, pre_ref, flat, bias_ref, band, blocks, whole, mine, kept, theirs, part, landed, res,
             w_sem, in_sem, pre_sem, bias_sem, in_send, in_recv, inx_send, inx_recv, px_send, px_recv,
             part_send, part_recv, res_send, res_recv, rx_send, rx_recv):
    n, w = lax.axis_index("narrow"), lax.axis_index("wide")
    core, pair = rem(n, 2), div(n, 2)
    other, chip, pairs = 1 - core, pair * wide + w, narrow // 2
    chips = pairs * wide
    rows, width = whole.shape
    half = width // 2
    cols = half // LANES
    tall = part.shape[1]
    block_rows, block_cols = in_ref.shape
    depth, edge = wide // 2, wide // 4
    owners = pairs * depth
    rounds = -(-pieces // owners)

    def peers(body):
        if chips <= 16:
            along = [rem(pair + a, pairs) * 2 + core for a in range(pairs)]
            across = [rem(w + b, wide) for b in range(wide)]
            for b in (*range(edge + 1, wide), *range(edge + 1)):
                for a in reversed(range(pairs)):
                    if a or b:
                        body({"narrow": along[a], "wide": across[b]}, a, b)
        else:
            def one(i):
                a, b = div(i, wide), rem(i, wide)
                body({"narrow": rem(pair + a, pairs) * 2 + core, "wide": rem(w + b, wide)}, a, b)
            each(1, chips, one)

    partner = {"narrow": pair * 2 + other, "wide": w}
    middle = (w >= edge) & (w < edge + depth)
    seat = pair * depth + lax.min(lax.max(w - edge, 0), depth - 1)
    held = [middle & (seat + r * owners < pieces) for r in range(rounds)]
    owned = [lax.min(seat + r * owners, pieces - 1) for r in range(rounds)]

    def by_count(body):
        for count in range(rounds + 1):
            at_least = held[count - 1] if count else None
            below = jnp.logical_not(held[count]) if count < rounds else None
            both = below if at_least is None else at_least if below is None else at_least & below
            pl.when(both)(functools.partial(body, count))

    def assembled(h):
        return jnp.concatenate([jnp.concatenate([
            res[h, q * cols + j] for j in range(cols)], axis=1) for q in range(pieces // cols)], axis=0)

    def columns(h):
        return pl.ds(pl.multiple_of(h * half, LANES), half)

    def load(h, slot):
        return pltpu.make_async_copy(w_hbm.at[:, columns(h)], w_ref.at[slot], w_sem.at[slot])

    barrier = pltpu.get_barrier_semaphore()
    def greet(to, a, b):
        def signal():
            pl.semaphore_signal(barrier, inc=1, device_id=to, device_id_type=MESH)

        if isinstance(a, int) and (a == 0 or b == 0):
            signal()
        else:
            there = (to["wide"] >= edge) & (to["wide"] < edge + depth)
            pl.when(middle | there | (a == 0) | (b == 0))(signal)

    peers(greet)
    for a in range(pairs):
        pl.semaphore_signal(barrier, inc=1, device_id_type=MESH, device_id={
            "narrow": rem(pair + a, pairs) * 2 + other, "wide": w})

    small = [pltpu.make_async_copy(in_hbm, in_ref, in_sem),
             pltpu.make_async_copy(pre_hbm, pre_ref, pre_sem),
             pltpu.make_async_copy(bias_hbm, flat, bias_sem)]
    for copy in small:
        copy.start()
    load(other, 0).start()
    load(core, 1).start()

    for copy in small:
        copy.wait()
    block = in_ref[...]
    blocks[n, w] = block
    bias_ref[...] = flat[...].reshape(1, width)
    for a in range(narrow):
        for b in range(8 // block_rows):
            band[b * block_rows:(b + 1) * block_rows, a * block_cols:(a + 1) * block_cols] = block.astype(F32)

    def placed(h):
        repeated = jnp.concatenate([band[:, columns(h)]] * (rows // 8), axis=0)
        row = lax.broadcasted_iota(jnp.int32, (rows, half), 0) - w * block_rows
        col = lax.broadcasted_iota(jnp.int32, (rows, half), 1) + (h * half - n * block_cols)
        inside = (row >= 0) & (row < block_rows) & (col >= 0) & (col < block_cols)
        return jnp.where(inside, repeated, 0.0)

    hidden = jnp.maximum(pre_ref[...], jnp.zeros_like(pre_ref))
    load(other, 0).wait()
    sent = jnp.dot(hidden, w_ref[0], preferred_element_type=F32) - placed(other)
    step = mine.shape[2]
    for i in range(mine.shape[0]):
        mine[i] = sent[:, i * step:(i + 1) * step]
    load(core, 1).wait()
    kept[...] = jnp.dot(hidden, w_ref[1], preferred_element_type=F32) - placed(core)

    @pl.when(middle)
    def _():
        pl.semaphore_wait(barrier, pairs + chips - 1)

    @pl.when(jnp.logical_not(middle))
    def _():
        pl.semaphore_wait(barrier, pairs + owners + wide - depth - 1 + pairs - 1)

    cuts = mine.shape[0]
    swaps = [pltpu.make_async_remote_copy(
        src_ref=mine.at[i], dst_ref=theirs.at[i], send_sem=px_send.at[i], recv_sem=px_recv.at[i],
        device_id=partner, device_id_type=MESH) for i in range(cuts)]
    for swap in swaps:
        swap.start()

    def send_block(b):
        pltpu.make_async_remote_copy(
            src_ref=in_ref, dst_ref=blocks.at[n, w], send_sem=in_send, recv_sem=in_recv,
            device_id={"narrow": n, "wide": rem(w + b, wide)}, device_id_type=MESH).start()

    each(1, wide, send_block)
    def send_part(k):
        spot, r = rem(k, owners), div(k, owners)
        row, to_wide = div(spot, depth), edge + rem(spot, depth)

        @pl.when(row * wide + to_wide != chip)
        def _():
            pltpu.make_async_remote_copy(
                src_ref=part.at[k], dst_ref=landed.at[r, chip], send_sem=part_send, recv_sem=part_recv.at[r],
                device_id={"narrow": row * 2 + core, "wide": to_wide}, device_id_type=MESH).start()

    for i in range(cuts):
        swaps[i].wait_recv()
        total = (kept[:, i * step:(i + 1) * step] + theirs[i]).astype(BF16)
        for k in range(pieces):
            q, j = k // cols, k % cols - i * step // LANES
            if 0 <= j < step // LANES:
                part[k] = total[q * tall:(q + 1) * tall, j * LANES:(j + 1) * LANES]
                send_part(k)
    wait_bytes(blocks.at[n, pl.ds(0, wide - 1)], in_recv)

    def send_blocks(a):
        pltpu.make_async_remote_copy(
            src_ref=blocks.at[n], dst_ref=blocks.at[n], send_sem=inx_send, recv_sem=inx_recv,
            device_id={"narrow": rem(n + a, narrow), "wide": w}, device_id_type=MESH).start()

    each(1, narrow, send_blocks)
    hid_ref[...] = hidden.astype(F32).T.astype(BF16)

    def finish(r):
        own = owned[r]
        landed[r, chip] = part[own]
        wait_bytes(landed.at[r, pl.ds(0, chips - 1)], part_recv.at[r])
        reduced = jnp.sum(landed[r].astype(F32), axis=0)
        at = pl.ds(pl.multiple_of(core * half + rem(own, cols) * LANES, LANES), LANES)
        res[core, own] = (reduced + bias_ref[:, at]).astype(BF16)

        def send_res(to, a, b):
            pltpu.make_async_remote_copy(
                src_ref=res.at[core, own], dst_ref=res.at[core, own], send_sem=res_send.at[r],
                recv_sem=res_recv, device_id=to, device_id_type=MESH).start()

        peers(send_res)

    for r in range(rounds):
        pl.when(held[r])(functools.partial(finish, r))

    wait_bytes(blocks.at[pl.ds(0, narrow - 1)], inx_recv)
    for a in range(narrow):
        for b in range(wide):
            whole[b * block_rows:(b + 1) * block_rows, a * block_cols:(a + 1) * block_cols] = (
                blocks[a, b].astype(F32))
    cent_ref[...] = (whole[...] - bias_ref[...]).T.astype(BF16)

    by_count(lambda count: wait_bytes(res.at[core, pl.ds(0, pieces - count)], res_recv))
    last = pltpu.make_async_remote_copy(
        src_ref=res.at[core], dst_ref=res.at[core], send_sem=rx_send, recv_sem=rx_recv,
        device_id=partner, device_id_type=MESH)
    last.start()
    first = assembled(core)
    dec_ref[...] = jnp.dot(hid_ref[...], first, preferred_element_type=F32).astype(BF16)
    back_ref[...] = lax.dot_general(first, w_ref[1], (((1,), (1,)), ((), ())), preferred_element_type=F32)
    for swap in swaps:
        swap.wait_send()
    wait_bytes(blocks.at[n, pl.ds(0, wide - 1)], in_send)
    wait_bytes(blocks.at[pl.ds(0, narrow - 1)], inx_send)

    by_count(lambda count: wait_bytes(part.at[pl.ds(0, pieces - count)], part_send))
    for r in range(rounds):
        pl.when(held[r])(functools.partial(
            wait_bytes, landed.at[r, pl.ds(0, chips - 1)], res_send.at[r]))
    last.wait()
    resid_ref[...] = assembled(other)


def gradients(hid_ref, resid_ref, cent_ref, dec_ref, back_ref, pre_ref, w_ref, enc_hbm, dec_hbm,
              enc, dec, enc_sem, dec_sem):
    core = rem(lax.axis_index("narrow"), 2)
    half = resid_ref.shape[1]

    def columns(h):
        return pl.ds(pl.multiple_of(h * half, LANES), half)

    copies = [pltpu.make_async_copy(dec_ref, dec_hbm.at[:, columns(core)], dec_sem.at[0])]
    copies[0].start()
    backward = back_ref[...] + lax.dot_general(
        resid_ref[...], w_ref[:, columns(1 - core)], (((1,), (1,)), ((), ())), preferred_element_type=F32)
    masked = jnp.where(pre_ref[...].astype(F32) > 0, backward, 0.0).astype(BF16)
    dec[...] = jnp.dot(hid_ref[...], resid_ref[...], preferred_element_type=F32).astype(BF16)
    copies.append(pltpu.make_async_copy(dec, dec_hbm.at[:, columns(1 - core)], dec_sem.at[1]))
    copies[1].start()
    cuts = enc_sem.shape[0]
    step = enc.shape[0] // cuts
    for i in range(cuts):
        span = slice(i * step, (i + 1) * step)
        enc[span, :] = jnp.dot(
            cent_ref[span, :], masked, preferred_element_type=F32).astype(BF16)
        copies.append(pltpu.make_async_copy(enc.at[span, :], enc_hbm.at[span, :], enc_sem.at[i]))
        copies[-1].start()
    for copy in copies:
        copy.wait()


def shards(narrow, wide, inputs, decoder_bias, preactivations, decoder_weight):
    rows, features = preactivations.shape
    width = decoder_weight.shape[1]
    half, chips = width // 2, (narrow // 2) * wide
    cols = half // LANES
    groups = 1
    while cols * groups * 2 <= chips and rows % (groups * 2 * 16) == 0:
        groups *= 2
    pieces, tall = cols * groups, rows // groups
    cuts = 3 if cols % 3 == 0 else 1
    rounds = -(-pieces // (narrow // 2 * (wide // 2)))
    vmem, hbm = pl.BlockSpec(memory_space=pltpu.VMEM), pl.BlockSpec(memory_space=pltpu.HBM)
    dma = pltpu.SemaphoreType.DMA
    kept = pl.pallas_call(
        functools.partial(exchange, narrow, wide, pieces),
        out_shape=(jax.ShapeDtypeStruct((rows, half), BF16),
                   jax.ShapeDtypeStruct((width, rows), BF16),
                   jax.ShapeDtypeStruct((features, rows), BF16),
                   jax.ShapeDtypeStruct((features, half), BF16),
                   jax.ShapeDtypeStruct((rows, features), F32)),
        in_specs=[hbm] * 4,
        out_specs=(vmem,) * 5,
        scratch_shapes=[
            pltpu.VMEM((2, features, half), BF16),
            pltpu.VMEM(inputs.shape, BF16),
            pltpu.VMEM((rows, features), BF16),
            pltpu.VMEM((width,), F32),
            pltpu.VMEM((1, width), F32),
            pltpu.VMEM((8, width), F32),
            pltpu.VMEM((narrow, wide) + inputs.shape, BF16),
            pltpu.VMEM((rows, width), F32),
            pltpu.VMEM((cuts, rows, half // cuts), F32),
            pltpu.VMEM((rows, half), F32),
            pltpu.VMEM((cuts, rows, half // cuts), F32),
            pltpu.VMEM((pieces, tall, LANES), BF16),
            pltpu.VMEM((rounds, chips, tall, LANES), BF16),
            pltpu.VMEM((2, pieces, tall, LANES), BF16),
            dma((2,)),
        ] + [dma] * 7 + [dma((cuts,)), dma((cuts,)), dma, dma((rounds,)), dma((rounds,)), dma, dma, dma],
        compiler_params=pltpu.CompilerParams(
            collective_id=0, has_side_effects=True, vmem_limit_bytes=32 * 2**20),
        name="exchange",
    )(*(pltpu.with_memory_space_constraint(x, pltpu.HBM)
        for x in (inputs, decoder_bias, preactivations, decoder_weight)))
    resid, centered, hidden, decoder, backward = kept
    return pl.pallas_call(
        gradients,
        out_shape=(jax.ShapeDtypeStruct((width, features), BF16),
                   jax.ShapeDtypeStruct((features, width), BF16)),
        in_specs=[vmem] * 7,
        out_specs=(hbm, hbm),
        scratch_shapes=[
            pltpu.VMEM((width, features), BF16),
            pltpu.VMEM((features, half), BF16),
            dma((3,)), dma((2,)),
        ],
        compiler_params=pltpu.CompilerParams(vmem_limit_bytes=32 * 2**20),
        name="gradients",
    )(hidden, resid, centered, decoder, backward, preactivations, decoder_weight)


def solution(mesh):
    placed = (P("wide", "narrow"), P(), P(None, ("narrow", "wide")), P(("narrow", "wide"), None))
    return jax.shard_map(
        functools.partial(shards, mesh.shape["narrow"], mesh.shape["wide"]),
        mesh=mesh,
        in_specs=placed,
        out_specs=(P(None, ("narrow", "wide")), P(("narrow", "wide"), None)),
        check_vma=False,
    )
```

```python
import functools

import jax
import jax.numpy as jnp
from jax import lax
from jax.experimental import pallas as pl
from jax.experimental.pallas import tpu as pltpu
from jax.sharding import PartitionSpec as P

MESH = pl.DeviceIdType.MESH
LANES = 128
BF16 = jnp.bfloat16
F32 = jnp.float32


def each(low, high, body):
    if high - low <= 16:
        for i in range(low, high):
            body(i)
    else:
        lax.fori_loop(low, high, lambda i, _: (body(i), 0)[1], 0)


def div(a, b):
    return a // b if isinstance(a, int) else a if b == 1 else lax.div(a, jnp.int32(b))


def rem(a, b):
    return a % b if isinstance(a, int) else lax.rem(a, jnp.int32(b))


def wait_bytes(ref, sem):
    pltpu.make_async_copy(ref, ref, sem).wait()


def exchange(narrow, wide, pieces, in_hbm, bias_hbm, pre_hbm, w_hbm, resid_ref, cent_ref, hid_ref, dec_ref, back_ref,
             w_ref, in_ref, pre_ref, flat, bias_ref, band, blocks, whole, mine, kept, theirs, part, landed, res,
             w_sem, in_sem, pre_sem, bias_sem, in_send, in_recv, inx_send, inx_recv, px_send, px_recv,
             part_send, part_recv, res_send, res_recv, rx_send, rx_recv):
    n, w = lax.axis_index("narrow"), lax.axis_index("wide")
    core, pair = rem(n, 2), div(n, 2)
    other, chip, pairs = 1 - core, pair * wide + w, narrow // 2
    chips = pairs * wide
    rows, width = whole.shape
    half = width // 2
    cols = half // LANES
    tall = part.shape[1]
    block_rows, block_cols = in_ref.shape
    depth, edge = wide // 2, wide // 4
    owners = pairs * depth
    rounds = -(-pieces // owners)

    def peers(body):
        if chips <= 16:
            along = [rem(pair + a, pairs) * 2 + core for a in range(pairs)]
            across = [rem(w + b, wide) for b in range(wide)]
            for b in (*range(edge + 1, wide), *range(edge + 1)):
                for a in reversed(range(pairs)):
                    if a or b:
                        body({"narrow": along[a], "wide": across[b]}, a, b)
        else:
            def one(i):
                a, b = div(i, wide), rem(i, wide)
                body({"narrow": rem(pair + a, pairs) * 2 + core, "wide": rem(w + b, wide)}, a, b)
            each(1, chips, one)

    partner = {"narrow": pair * 2 + other, "wide": w}
    middle = (w >= edge) & (w < edge + depth)
    seat = pair * depth + lax.min(lax.max(w - edge, 0), depth - 1)
    held = [middle & (seat + r * owners < pieces) for r in range(rounds)]
    owned = [lax.min(seat + r * owners, pieces - 1) for r in range(rounds)]

    def by_count(body):
        for count in range(rounds + 1):
            at_least = held[count - 1] if count else None
            below = jnp.logical_not(held[count]) if count < rounds else None
            both = below if at_least is None else at_least if below is None else at_least & below
            pl.when(both)(functools.partial(body, count))

    def assembled(h):
        return jnp.concatenate([jnp.concatenate([
            res[h, q * cols + j] for j in range(cols)], axis=1) for q in range(pieces // cols)], axis=0)

    def columns(h):
        return pl.ds(pl.multiple_of(h * half, LANES), half)

    def load(h, slot):
        return pltpu.make_async_copy(w_hbm.at[:, columns(h)], w_ref.at[slot], w_sem.at[slot])

    barrier = pltpu.get_barrier_semaphore()
    def greet(to, a, b):
        def signal():
            pl.semaphore_signal(barrier, inc=1, device_id=to, device_id_type=MESH)

        if isinstance(a, int) and (a == 0 or b == 0):
            signal()
        else:
            there = (to["wide"] >= edge) & (to["wide"] < edge + depth)
            pl.when(middle | there | (a == 0) | (b == 0))(signal)

    peers(greet)
    for a in range(pairs):
        pl.semaphore_signal(barrier, inc=1, device_id_type=MESH, device_id={
            "narrow": rem(pair + a, pairs) * 2 + other, "wide": w})

    small = [pltpu.make_async_copy(in_hbm, in_ref, in_sem),
             pltpu.make_async_copy(pre_hbm, pre_ref, pre_sem),
             pltpu.make_async_copy(bias_hbm, flat, bias_sem)]
    for copy in small:
        copy.start()
    load(other, 0).start()
    load(core, 1).start()

    for copy in small:
        copy.wait()
    block = in_ref[...]
    blocks[n, w] = block
    bias_ref[...] = flat[...].reshape(1, width)
    for a in range(narrow):
        for b in range(8 // block_rows):
            band[b * block_rows:(b + 1) * block_rows, a * block_cols:(a + 1) * block_cols] = block.astype(F32)

    def placed(h):
        repeated = jnp.concatenate([band[:, columns(h)]] * (rows // 8), axis=0)
        row = lax.broadcasted_iota(jnp.int32, (rows, half), 0) - w * block_rows
        col = lax.broadcasted_iota(jnp.int32, (rows, half), 1) + (h * half - n * block_cols)
        inside = (row >= 0) & (row < block_rows) & (col >= 0) & (col < block_cols)
        return jnp.where(inside, repeated, 0.0)

    hidden = jnp.maximum(pre_ref[...], jnp.zeros_like(pre_ref))
    load(other, 0).wait()
    sent = jnp.dot(hidden, w_ref[0], preferred_element_type=F32) - placed(other)
    step = mine.shape[2]
    for i in range(mine.shape[0]):
        mine[i] = sent[:, i * step:(i + 1) * step]
    load(core, 1).wait()
    kept[...] = jnp.dot(hidden, w_ref[1], preferred_element_type=F32) - placed(core)

    @pl.when(middle)
    def _():
        pl.semaphore_wait(barrier, pairs + chips - 1)

    @pl.when(jnp.logical_not(middle))
    def _():
        pl.semaphore_wait(barrier, pairs + owners + wide - depth - 1 + pairs - 1)

    cuts = mine.shape[0]
    swaps = [pltpu.make_async_remote_copy(
        src_ref=mine.at[i], dst_ref=theirs.at[i], send_sem=px_send.at[i], recv_sem=px_recv.at[i],
        device_id=partner, device_id_type=MESH) for i in range(cuts)]
    for swap in swaps:
        swap.start()

    def send_block(b):
        pltpu.make_async_remote_copy(
            src_ref=in_ref, dst_ref=blocks.at[n, w], send_sem=in_send, recv_sem=in_recv,
            device_id={"narrow": n, "wide": rem(w + b, wide)}, device_id_type=MESH).start()

    each(1, wide, send_block)
    def send_part(k):
        spot, r = rem(k, owners), div(k, owners)
        row, to_wide = div(spot, depth), edge + rem(spot, depth)

        @pl.when(row * wide + to_wide != chip)
        def _():
            pltpu.make_async_remote_copy(
                src_ref=part.at[k], dst_ref=landed.at[r, chip], send_sem=part_send, recv_sem=part_recv.at[r],
                device_id={"narrow": row * 2 + core, "wide": to_wide}, device_id_type=MESH).start()

    for i in range(cuts):
        swaps[i].wait_recv()
        total = (kept[:, i * step:(i + 1) * step] + theirs[i]).astype(BF16)
        for k in range(pieces):
            q, j = k // cols, k % cols - i * step // LANES
            if 0 <= j < step // LANES:
                part[k] = total[q * tall:(q + 1) * tall, j * LANES:(j + 1) * LANES]
                send_part(k)
    wait_bytes(blocks.at[n, pl.ds(0, wide - 1)], in_recv)

    def send_blocks(a):
        pltpu.make_async_remote_copy(
            src_ref=blocks.at[n], dst_ref=blocks.at[n], send_sem=inx_send, recv_sem=inx_recv,
            device_id={"narrow": rem(n + a, narrow), "wide": w}, device_id_type=MESH).start()

    each(1, narrow, send_blocks)
    hid_ref[...] = hidden.astype(F32).T.astype(BF16)

    def finish(r):
        own = owned[r]
        landed[r, chip] = part[own]
        wait_bytes(landed.at[r, pl.ds(0, chips - 1)], part_recv.at[r])
        reduced = jnp.sum(landed[r].astype(F32), axis=0)
        at = pl.ds(pl.multiple_of(core * half + rem(own, cols) * LANES, LANES), LANES)
        res[core, own] = (reduced + bias_ref[:, at]).astype(BF16)

        def send_res(to, a, b):
            pltpu.make_async_remote_copy(
                src_ref=res.at[core, own], dst_ref=res.at[core, own], send_sem=res_send.at[r],
                recv_sem=res_recv, device_id=to, device_id_type=MESH).start()

        peers(send_res)

    for r in range(rounds):
        pl.when(held[r])(functools.partial(finish, r))

    by_count(lambda count: wait_bytes(res.at[core, pl.ds(0, pieces - count)], res_recv))
    last = pltpu.make_async_remote_copy(
        src_ref=res.at[core], dst_ref=res.at[core], send_sem=rx_send, recv_sem=rx_recv,
        device_id=partner, device_id_type=MESH)
    last.start()
    first = assembled(core)
    dec_ref[...] = jnp.dot(hid_ref[...], first, preferred_element_type=F32).astype(BF16)
    back_ref[...] = lax.dot_general(first, w_ref[1], (((1,), (1,)), ((), ())), preferred_element_type=F32)

    wait_bytes(blocks.at[pl.ds(0, narrow - 1)], inx_recv)
    for a in range(narrow):
        for b in range(wide):
            whole[b * block_rows:(b + 1) * block_rows, a * block_cols:(a + 1) * block_cols] = (
                blocks[a, b].astype(F32))
    cent_ref[...] = (whole[...] - bias_ref[...]).T.astype(BF16)
    for swap in swaps:
        swap.wait_send()
    wait_bytes(blocks.at[n, pl.ds(0, wide - 1)], in_send)
    wait_bytes(blocks.at[pl.ds(0, narrow - 1)], inx_send)

    by_count(lambda count: wait_bytes(part.at[pl.ds(0, pieces - count)], part_send))
    for r in range(rounds):
        pl.when(held[r])(functools.partial(
            wait_bytes, landed.at[r, pl.ds(0, chips - 1)], res_send.at[r]))
    last.wait()
    resid_ref[...] = assembled(other)


def gradients(hid_ref, resid_ref, cent_ref, dec_ref, back_ref, pre_ref, w_ref, enc_hbm, dec_hbm,
              enc, dec, enc_sem, dec_sem):
    core = rem(lax.axis_index("narrow"), 2)
    half = resid_ref.shape[1]

    def columns(h):
        return pl.ds(pl.multiple_of(h * half, LANES), half)

    copies = [pltpu.make_async_copy(dec_ref, dec_hbm.at[:, columns(core)], dec_sem.at[0])]
    copies[0].start()
    backward = back_ref[...] + lax.dot_general(
        resid_ref[...], w_ref[:, columns(1 - core)], (((1,), (1,)), ((), ())), preferred_element_type=F32)
    masked = jnp.where(pre_ref[...].astype(F32) > 0, backward, 0.0).astype(BF16)
    dec[...] = jnp.dot(hid_ref[...], resid_ref[...], preferred_element_type=F32).astype(BF16)
    copies.append(pltpu.make_async_copy(dec, dec_hbm.at[:, columns(1 - core)], dec_sem.at[1]))
    copies[1].start()
    cuts = enc_sem.shape[0]
    step = enc.shape[0] // cuts
    for i in range(cuts):
        span = slice(i * step, (i + 1) * step)
        enc[span, :] = jnp.dot(
            cent_ref[span, :], masked, preferred_element_type=F32).astype(BF16)
        copies.append(pltpu.make_async_copy(enc.at[span, :], enc_hbm.at[span, :], enc_sem.at[i]))
        copies[-1].start()
    for copy in copies:
        copy.wait()


def shards(narrow, wide, inputs, decoder_bias, preactivations, decoder_weight):
    rows, features = preactivations.shape
    width = decoder_weight.shape[1]
    half, chips = width // 2, (narrow // 2) * wide
    cols = half // LANES
    groups = 1
    while cols * groups * 2 <= chips and rows % (groups * 2 * 16) == 0:
        groups *= 2
    pieces, tall = cols * groups, rows // groups
    cuts = 3 if cols % 3 == 0 else 1
    rounds = -(-pieces // (narrow // 2 * (wide // 2)))
    vmem, hbm = pl.BlockSpec(memory_space=pltpu.VMEM), pl.BlockSpec(memory_space=pltpu.HBM)
    dma = pltpu.SemaphoreType.DMA
    kept = pl.pallas_call(
        functools.partial(exchange, narrow, wide, pieces),
        out_shape=(jax.ShapeDtypeStruct((rows, half), BF16),
                   jax.ShapeDtypeStruct((width, rows), BF16),
                   jax.ShapeDtypeStruct((features, rows), BF16),
                   jax.ShapeDtypeStruct((features, half), BF16),
                   jax.ShapeDtypeStruct((rows, features), F32)),
        in_specs=[hbm] * 4,
        out_specs=(vmem,) * 5,
        scratch_shapes=[
            pltpu.VMEM((2, features, half), BF16),
            pltpu.VMEM(inputs.shape, BF16),
            pltpu.VMEM((rows, features), BF16),
            pltpu.VMEM((width,), F32),
            pltpu.VMEM((1, width), F32),
            pltpu.VMEM((8, width), F32),
            pltpu.VMEM((narrow, wide) + inputs.shape, BF16),
            pltpu.VMEM((rows, width), F32),
            pltpu.VMEM((cuts, rows, half // cuts), F32),
            pltpu.VMEM((rows, half), F32),
            pltpu.VMEM((cuts, rows, half // cuts), F32),
            pltpu.VMEM((pieces, tall, LANES), BF16),
            pltpu.VMEM((rounds, chips, tall, LANES), BF16),
            pltpu.VMEM((2, pieces, tall, LANES), BF16),
            dma((2,)),
        ] + [dma] * 7 + [dma((cuts,)), dma((cuts,)), dma, dma((rounds,)), dma((rounds,)), dma, dma, dma],
        compiler_params=pltpu.CompilerParams(
            collective_id=0, has_side_effects=True, vmem_limit_bytes=32 * 2**20),
        name="exchange",
    )(*(pltpu.with_memory_space_constraint(x, pltpu.HBM)
        for x in (inputs, decoder_bias, preactivations, decoder_weight)))
    resid, centered, hidden, decoder, backward = kept
    return pl.pallas_call(
        gradients,
        out_shape=(jax.ShapeDtypeStruct((width, features), BF16),
                   jax.ShapeDtypeStruct((features, width), BF16)),
        in_specs=[vmem] * 7,
        out_specs=(hbm, hbm),
        scratch_shapes=[
            pltpu.VMEM((width, features), BF16),
            pltpu.VMEM((features, half), BF16),
            dma((3,)), dma((2,)),
        ],
        compiler_params=pltpu.CompilerParams(vmem_limit_bytes=32 * 2**20),
        name="gradients",
    )(hidden, resid, centered, decoder, backward, preactivations, decoder_weight)


def solution(mesh):
    placed = (P("wide", "narrow"), P(), P(None, ("narrow", "wide")), P(("narrow", "wide"), None))
    return jax.shard_map(
        functools.partial(shards, mesh.shape["narrow"], mesh.shape["wide"]),
        mesh=mesh,
        in_specs=placed,
        out_specs=(P(None, ("narrow", "wide")), P(("narrow", "wide"), None)),
        check_vma=False,
    )
```

```python
import functools

import jax
import jax.numpy as jnp
from jax import lax
from jax.experimental import pallas as pl
from jax.experimental.pallas import tpu as pltpu
from jax.sharding import PartitionSpec as P

MESH = pl.DeviceIdType.MESH
LANES = 128
BF16 = jnp.bfloat16
F32 = jnp.float32


def each(low, high, body):
    if high - low <= 16:
        for i in range(low, high):
            body(i)
    else:
        lax.fori_loop(low, high, lambda i, _: (body(i), 0)[1], 0)


def div(a, b):
    return a // b if isinstance(a, int) else a if b == 1 else lax.div(a, jnp.int32(b))


def rem(a, b):
    return a % b if isinstance(a, int) else lax.rem(a, jnp.int32(b))


def wait_bytes(ref, sem):
    pltpu.make_async_copy(ref, ref, sem).wait()


def exchange(narrow, wide, pieces, in_hbm, bias_hbm, pre_hbm, w_hbm, resid_ref, cent_ref, hid_ref, dec_ref, back_ref,
             w_ref, in_ref, pre_ref, flat, bias_ref, band, blocks, whole, mine, kept, theirs, part, landed, res,
             w_sem, in_sem, pre_sem, bias_sem, in_send, in_recv, inx_send, inx_recv, px_send, px_recv,
             part_send, part_recv, res_send, res_recv, rx_send, rx_recv):
    n, w = lax.axis_index("narrow"), lax.axis_index("wide")
    core, pair = rem(n, 2), div(n, 2)
    other, chip, pairs = 1 - core, pair * wide + w, narrow // 2
    chips = pairs * wide
    rows, width = whole.shape
    half = width // 2
    cols = half // LANES
    tall = part.shape[1]
    block_rows, block_cols = in_ref.shape
    depth, edge = wide // 2, wide // 4
    owners = pairs * depth
    rounds = -(-pieces // owners)

    def peers(body):
        if chips <= 16:
            along = [rem(pair + a, pairs) * 2 + core for a in range(pairs)]
            across = [rem(w + b, wide) for b in range(wide)]
            for b in (*range(edge + 1, wide), *range(edge + 1)):
                for a in reversed(range(pairs)):
                    if a or b:
                        body({"narrow": along[a], "wide": across[b]}, a, b)
        else:
            def one(i):
                a, b = div(i, wide), rem(i, wide)
                body({"narrow": rem(pair + a, pairs) * 2 + core, "wide": rem(w + b, wide)}, a, b)
            each(1, chips, one)

    partner = {"narrow": pair * 2 + other, "wide": w}
    middle = (w >= edge) & (w < edge + depth)
    seat = pair * depth + lax.min(lax.max(w - edge, 0), depth - 1)
    held = [middle & (seat + r * owners < pieces) for r in range(rounds)]
    owned = [lax.min(seat + r * owners, pieces - 1) for r in range(rounds)]

    def by_count(body):
        for count in range(rounds + 1):
            at_least = held[count - 1] if count else None
            below = jnp.logical_not(held[count]) if count < rounds else None
            both = below if at_least is None else at_least if below is None else at_least & below
            pl.when(both)(functools.partial(body, count))

    def assembled(h):
        return jnp.concatenate([jnp.concatenate([
            res[h, q * cols + j] for j in range(cols)], axis=1) for q in range(pieces // cols)], axis=0)

    def columns(h):
        return pl.ds(pl.multiple_of(h * half, LANES), half)

    def load(h, slot):
        return pltpu.make_async_copy(w_hbm.at[:, columns(h)], w_ref.at[slot], w_sem.at[slot])

    barrier = pltpu.get_barrier_semaphore()
    def greet(to, a, b):
        def signal():
            pl.semaphore_signal(barrier, inc=1, device_id=to, device_id_type=MESH)

        if isinstance(a, int) and (a == 0 or b == 0):
            signal()
        else:
            there = (to["wide"] >= edge) & (to["wide"] < edge + depth)
            pl.when(middle | there | (a == 0) | (b == 0))(signal)

    peers(greet)
    for a in range(pairs):
        pl.semaphore_signal(barrier, inc=1, device_id_type=MESH, device_id={
            "narrow": rem(pair + a, pairs) * 2 + other, "wide": w})

    small = [pltpu.make_async_copy(in_hbm, in_ref, in_sem),
             pltpu.make_async_copy(pre_hbm, pre_ref, pre_sem),
             pltpu.make_async_copy(bias_hbm, flat, bias_sem)]
    for copy in small:
        copy.start()
    load(other, 0).start()
    load(core, 1).start()

    for copy in small:
        copy.wait()
    block = in_ref[...]
    blocks[n, w] = block
    bias_ref[...] = flat[...].reshape(1, width)
    for a in range(narrow):
        for b in range(8 // block_rows):
            band[b * block_rows:(b + 1) * block_rows, a * block_cols:(a + 1) * block_cols] = block.astype(F32)

    def placed(h):
        repeated = jnp.concatenate([band[:, columns(h)]] * (rows // 8), axis=0)
        row = lax.broadcasted_iota(jnp.int32, (rows, half), 0) - w * block_rows
        col = lax.broadcasted_iota(jnp.int32, (rows, half), 1) + (h * half - n * block_cols)
        inside = (row >= 0) & (row < block_rows) & (col >= 0) & (col < block_cols)
        return jnp.where(inside, repeated, 0.0)

    hidden = jnp.maximum(pre_ref[...], jnp.zeros_like(pre_ref))
    load(other, 0).wait()
    sent = jnp.dot(hidden, w_ref[0], preferred_element_type=F32) - placed(other)
    step = mine.shape[2]
    for i in range(mine.shape[0]):
        mine[i] = sent[:, i * step:(i + 1) * step]
    load(core, 1).wait()
    kept[...] = jnp.dot(hidden, w_ref[1], preferred_element_type=F32) - placed(core)

    @pl.when(middle)
    def _():
        pl.semaphore_wait(barrier, pairs + chips - 1)

    @pl.when(jnp.logical_not(middle))
    def _():
        pl.semaphore_wait(barrier, pairs + owners + wide - depth - 1 + pairs - 1)

    cuts = mine.shape[0]
    swaps = [pltpu.make_async_remote_copy(
        src_ref=mine.at[i], dst_ref=theirs.at[i], send_sem=px_send.at[i], recv_sem=px_recv.at[i],
        device_id=partner, device_id_type=MESH) for i in range(cuts)]
    for swap in swaps:
        swap.start()

    def send_block(b):
        pltpu.make_async_remote_copy(
            src_ref=in_ref, dst_ref=blocks.at[n, w], send_sem=in_send, recv_sem=in_recv,
            device_id={"narrow": n, "wide": rem(w + b, wide)}, device_id_type=MESH).start()

    each(1, wide, send_block)
    def send_part(k):
        spot, r = rem(k, owners), div(k, owners)
        row, to_wide = div(spot, depth), edge + rem(spot, depth)

        @pl.when(row * wide + to_wide != chip)
        def _():
            pltpu.make_async_remote_copy(
                src_ref=part.at[k], dst_ref=landed.at[r, chip], send_sem=part_send, recv_sem=part_recv.at[r],
                device_id={"narrow": row * 2 + core, "wide": to_wide}, device_id_type=MESH).start()

    for i in range(cuts):
        swaps[i].wait_recv()
        total = (kept[:, i * step:(i + 1) * step] + theirs[i]).astype(BF16)
        for k in range(pieces):
            q, j = k // cols, k % cols - i * step // LANES
            if 0 <= j < step // LANES:
                part[k] = total[q * tall:(q + 1) * tall, j * LANES:(j + 1) * LANES]
                send_part(k)
    wait_bytes(blocks.at[n, pl.ds(0, wide - 1)], in_recv)

    def send_blocks(a):
        pltpu.make_async_remote_copy(
            src_ref=blocks.at[n], dst_ref=blocks.at[n], send_sem=inx_send, recv_sem=inx_recv,
            device_id={"narrow": rem(n + a, narrow), "wide": w}, device_id_type=MESH).start()

    pl.when(jnp.logical_not(middle))(lambda: each(1, narrow, send_blocks))
    hid_ref[...] = hidden.astype(F32).T.astype(BF16)

    def finish(r):
        own = owned[r]
        landed[r, chip] = part[own]
        wait_bytes(landed.at[r, pl.ds(0, chips - 1)], part_recv.at[r])
        reduced = jnp.sum(landed[r].astype(F32), axis=0)
        at = pl.ds(pl.multiple_of(core * half + rem(own, cols) * LANES, LANES), LANES)
        res[core, own] = (reduced + bias_ref[:, at]).astype(BF16)

        def send_res(to, a, b):
            pltpu.make_async_remote_copy(
                src_ref=res.at[core, own], dst_ref=res.at[core, own], send_sem=res_send.at[r],
                recv_sem=res_recv, device_id=to, device_id_type=MESH).start()

        peers(send_res)

    for r in range(rounds):
        pl.when(held[r])(functools.partial(finish, r))
    pl.when(middle)(lambda: each(1, narrow, send_blocks))

    by_count(lambda count: wait_bytes(res.at[core, pl.ds(0, pieces - count)], res_recv))
    last = pltpu.make_async_remote_copy(
        src_ref=res.at[core], dst_ref=res.at[core], send_sem=rx_send, recv_sem=rx_recv,
        device_id=partner, device_id_type=MESH)
    last.start()
    first = assembled(core)
    dec_ref[...] = jnp.dot(hid_ref[...], first, preferred_element_type=F32).astype(BF16)
    back_ref[...] = lax.dot_general(first, w_ref[1], (((1,), (1,)), ((), ())), preferred_element_type=F32)

    wait_bytes(blocks.at[pl.ds(0, narrow - 1)], inx_recv)
    for a in range(narrow):
        for b in range(wide):
            whole[b * block_rows:(b + 1) * block_rows, a * block_cols:(a + 1) * block_cols] = (
                blocks[a, b].astype(F32))
    cent_ref[...] = (whole[...] - bias_ref[...]).T.astype(BF16)
    for swap in swaps:
        swap.wait_send()
    wait_bytes(blocks.at[n, pl.ds(0, wide - 1)], in_send)
    wait_bytes(blocks.at[pl.ds(0, narrow - 1)], inx_send)

    by_count(lambda count: wait_bytes(part.at[pl.ds(0, pieces - count)], part_send))
    for r in range(rounds):
        pl.when(held[r])(functools.partial(
            wait_bytes, landed.at[r, pl.ds(0, chips - 1)], res_send.at[r]))
    last.wait()
    resid_ref[...] = assembled(other)


def gradients(hid_ref, resid_ref, cent_ref, dec_ref, back_ref, pre_ref, w_ref, enc_hbm, dec_hbm,
              enc, dec, enc_sem, dec_sem):
    core = rem(lax.axis_index("narrow"), 2)
    half = resid_ref.shape[1]

    def columns(h):
        return pl.ds(pl.multiple_of(h * half, LANES), half)

    copies = [pltpu.make_async_copy(dec_ref, dec_hbm.at[:, columns(core)], dec_sem.at[0])]
    copies[0].start()
    backward = back_ref[...] + lax.dot_general(
        resid_ref[...], w_ref[:, columns(1 - core)], (((1,), (1,)), ((), ())), preferred_element_type=F32)
    masked = jnp.where(pre_ref[...].astype(F32) > 0, backward, 0.0).astype(BF16)
    dec[...] = jnp.dot(hid_ref[...], resid_ref[...], preferred_element_type=F32).astype(BF16)
    copies.append(pltpu.make_async_copy(dec, dec_hbm.at[:, columns(1 - core)], dec_sem.at[1]))
    copies[1].start()
    cuts = enc_sem.shape[0]
    step = enc.shape[0] // cuts
    for i in range(cuts):
        span = slice(i * step, (i + 1) * step)
        enc[span, :] = jnp.dot(
            cent_ref[span, :], masked, preferred_element_type=F32).astype(BF16)
        copies.append(pltpu.make_async_copy(enc.at[span, :], enc_hbm.at[span, :], enc_sem.at[i]))
        copies[-1].start()
    for copy in copies:
        copy.wait()


def shards(narrow, wide, inputs, decoder_bias, preactivations, decoder_weight):
    rows, features = preactivations.shape
    width = decoder_weight.shape[1]
    half, chips = width // 2, (narrow // 2) * wide
    cols = half // LANES
    groups = 1
    while cols * groups * 2 <= chips and rows % (groups * 2 * 16) == 0:
        groups *= 2
    pieces, tall = cols * groups, rows // groups
    cuts = 3 if cols % 3 == 0 else 1
    rounds = -(-pieces // (narrow // 2 * (wide // 2)))
    vmem, hbm = pl.BlockSpec(memory_space=pltpu.VMEM), pl.BlockSpec(memory_space=pltpu.HBM)
    dma = pltpu.SemaphoreType.DMA
    kept = pl.pallas_call(
        functools.partial(exchange, narrow, wide, pieces),
        out_shape=(jax.ShapeDtypeStruct((rows, half), BF16),
                   jax.ShapeDtypeStruct((width, rows), BF16),
                   jax.ShapeDtypeStruct((features, rows), BF16),
                   jax.ShapeDtypeStruct((features, half), BF16),
                   jax.ShapeDtypeStruct((rows, features), F32)),
        in_specs=[hbm] * 4,
        out_specs=(vmem,) * 5,
        scratch_shapes=[
            pltpu.VMEM((2, features, half), BF16),
            pltpu.VMEM(inputs.shape, BF16),
            pltpu.VMEM((rows, features), BF16),
            pltpu.VMEM((width,), F32),
            pltpu.VMEM((1, width), F32),
            pltpu.VMEM((8, width), F32),
            pltpu.VMEM((narrow, wide) + inputs.shape, BF16),
            pltpu.VMEM((rows, width), F32),
            pltpu.VMEM((cuts, rows, half // cuts), F32),
            pltpu.VMEM((rows, half), F32),
            pltpu.VMEM((cuts, rows, half // cuts), F32),
            pltpu.VMEM((pieces, tall, LANES), BF16),
            pltpu.VMEM((rounds, chips, tall, LANES), BF16),
            pltpu.VMEM((2, pieces, tall, LANES), BF16),
            dma((2,)),
        ] + [dma] * 7 + [dma((cuts,)), dma((cuts,)), dma, dma((rounds,)), dma((rounds,)), dma, dma, dma],
        compiler_params=pltpu.CompilerParams(
            collective_id=0, has_side_effects=True, vmem_limit_bytes=32 * 2**20),
        name="exchange",
    )(*(pltpu.with_memory_space_constraint(x, pltpu.HBM)
        for x in (inputs, decoder_bias, preactivations, decoder_weight)))
    resid, centered, hidden, decoder, backward = kept
    return pl.pallas_call(
        gradients,
        out_shape=(jax.ShapeDtypeStruct((width, features), BF16),
                   jax.ShapeDtypeStruct((features, width), BF16)),
        in_specs=[vmem] * 7,
        out_specs=(hbm, hbm),
        scratch_shapes=[
            pltpu.VMEM((width, features), BF16),
            pltpu.VMEM((features, half), BF16),
            dma((3,)), dma((2,)),
        ],
        compiler_params=pltpu.CompilerParams(vmem_limit_bytes=32 * 2**20),
        name="gradients",
    )(hidden, resid, centered, decoder, backward, preactivations, decoder_weight)


def solution(mesh):
    placed = (P("wide", "narrow"), P(), P(None, ("narrow", "wide")), P(("narrow", "wide"), None))
    return jax.shard_map(
        functools.partial(shards, mesh.shape["narrow"], mesh.shape["wide"]),
        mesh=mesh,
        in_specs=placed,
        out_specs=(P(None, ("narrow", "wide")), P(("narrow", "wide"), None)),
        check_vma=False,
    )
```

```python
import functools

import jax
import jax.numpy as jnp
from jax import lax
from jax.experimental import pallas as pl
from jax.experimental.pallas import tpu as pltpu
from jax.sharding import PartitionSpec as P

MESH = pl.DeviceIdType.MESH
LANES = 128
BF16 = jnp.bfloat16
F32 = jnp.float32


def each(low, high, body):
    if high - low <= 16:
        for i in range(low, high):
            body(i)
    else:
        lax.fori_loop(low, high, lambda i, _: (body(i), 0)[1], 0)


def div(a, b):
    return a // b if isinstance(a, int) else a if b == 1 else lax.div(a, jnp.int32(b))


def rem(a, b):
    return a % b if isinstance(a, int) else lax.rem(a, jnp.int32(b))


def wait_bytes(ref, sem):
    pltpu.make_async_copy(ref, ref, sem).wait()


def exchange(narrow, wide, pieces, in_hbm, bias_hbm, pre_hbm, w_hbm, resid_ref, cent_ref, hid_ref, dec_ref, back_ref,
             w_ref, in_ref, pre_ref, flat, bias_ref, band, blocks, whole, mine, kept, theirs, part, landed, res,
             w_sem, in_sem, pre_sem, bias_sem, in_send, in_recv, inx_send, inx_recv, px_send, px_recv,
             part_send, part_recv, res_send, res_recv, rx_send, rx_recv):
    n, w = lax.axis_index("narrow"), lax.axis_index("wide")
    core, pair = rem(n, 2), div(n, 2)
    other, chip, pairs = 1 - core, pair * wide + w, narrow // 2
    chips = pairs * wide
    rows, width = whole.shape
    half = width // 2
    cols = half // LANES
    tall = part.shape[1]
    block_rows, block_cols = in_ref.shape
    depth, edge = wide // 2, wide // 4
    owners = pairs * depth
    rounds = -(-pieces // owners)

    def peers(body):
        if chips <= 16:
            along = [rem(pair + a, pairs) * 2 + core for a in range(pairs)]
            across = [rem(w + b, wide) for b in range(wide)]
            for b in (*range(edge + 1, wide), *range(edge + 1)):
                for a in reversed(range(pairs)):
                    if a or b:
                        body({"narrow": along[a], "wide": across[b]}, a, b)
        else:
            def one(i):
                a, b = div(i, wide), rem(i, wide)
                body({"narrow": rem(pair + a, pairs) * 2 + core, "wide": rem(w + b, wide)}, a, b)
            each(1, chips, one)

    partner = {"narrow": pair * 2 + other, "wide": w}
    middle = (w >= edge) & (w < edge + depth)
    seat = pair * depth + lax.min(lax.max(w - edge, 0), depth - 1)
    held = [middle & (seat + r * owners < pieces) for r in range(rounds)]
    owned = [lax.min(seat + r * owners, pieces - 1) for r in range(rounds)]

    def by_count(body):
        for count in range(rounds + 1):
            at_least = held[count - 1] if count else None
            below = jnp.logical_not(held[count]) if count < rounds else None
            both = below if at_least is None else at_least if below is None else at_least & below
            pl.when(both)(functools.partial(body, count))

    def assembled(h):
        return jnp.concatenate([jnp.concatenate([
            res[h, q * cols + j] for j in range(cols)], axis=1) for q in range(pieces // cols)], axis=0)

    def columns(h):
        return pl.ds(pl.multiple_of(h * half, LANES), half)

    def load(h, slot):
        return pltpu.make_async_copy(w_hbm.at[:, columns(h)], w_ref.at[slot], w_sem.at[slot])

    barrier = pltpu.get_barrier_semaphore()
    def greet(to, a, b):
        def signal():
            pl.semaphore_signal(barrier, inc=1, device_id=to, device_id_type=MESH)

        if isinstance(a, int) and (a == 0 or b == 0):
            signal()
        else:
            there = (to["wide"] >= edge) & (to["wide"] < edge + depth)
            pl.when(middle | there | (a == 0) | (b == 0))(signal)

    peers(greet)
    for a in range(pairs):
        pl.semaphore_signal(barrier, inc=1, device_id_type=MESH, device_id={
            "narrow": rem(pair + a, pairs) * 2 + other, "wide": w})

    small = [pltpu.make_async_copy(in_hbm, in_ref, in_sem),
             pltpu.make_async_copy(pre_hbm, pre_ref, pre_sem),
             pltpu.make_async_copy(bias_hbm, flat, bias_sem)]
    for copy in small:
        copy.start()
    load(other, 0).start()
    load(core, 1).start()

    for copy in small:
        copy.wait()
    block = in_ref[...]
    blocks[n, w] = block
    bias_ref[...] = flat[...].reshape(1, width)
    for a in range(narrow):
        for b in range(8 // block_rows):
            band[b * block_rows:(b + 1) * block_rows, a * block_cols:(a + 1) * block_cols] = block.astype(F32)

    def placed(h):
        repeated = jnp.concatenate([band[:, columns(h)]] * (rows // 8), axis=0)
        row = lax.broadcasted_iota(jnp.int32, (rows, half), 0) - w * block_rows
        col = lax.broadcasted_iota(jnp.int32, (rows, half), 1) + (h * half - n * block_cols)
        inside = (row >= 0) & (row < block_rows) & (col >= 0) & (col < block_cols)
        return jnp.where(inside, repeated, 0.0)

    hidden = jnp.maximum(pre_ref[...], jnp.zeros_like(pre_ref))
    load(other, 0).wait()
    sent = jnp.dot(hidden, w_ref[0], preferred_element_type=F32) - placed(other)
    step = mine.shape[2]
    for i in range(mine.shape[0]):
        mine[i] = sent[:, i * step:(i + 1) * step]
    load(core, 1).wait()
    kept[...] = jnp.dot(hidden, w_ref[1], preferred_element_type=F32) - placed(core)

    @pl.when(middle)
    def _():
        pl.semaphore_wait(barrier, pairs + chips - 1)

    @pl.when(jnp.logical_not(middle))
    def _():
        pl.semaphore_wait(barrier, pairs + owners + wide - depth - 1 + pairs - 1)

    cuts = mine.shape[0]
    swaps = [pltpu.make_async_remote_copy(
        src_ref=mine.at[i], dst_ref=theirs.at[i], send_sem=px_send.at[i], recv_sem=px_recv.at[i],
        device_id=partner, device_id_type=MESH) for i in range(cuts)]
    for swap in swaps:
        swap.start()

    def send_block(b):
        pltpu.make_async_remote_copy(
            src_ref=in_ref, dst_ref=blocks.at[n, w], send_sem=in_send, recv_sem=in_recv,
            device_id={"narrow": n, "wide": rem(w + b, wide)}, device_id_type=MESH).start()


    def send_part(k):
        spot, r = rem(k, owners), div(k, owners)
        row, to_wide = div(spot, depth), edge + rem(spot, depth)

        @pl.when(row * wide + to_wide != chip)
        def _():
            pltpu.make_async_remote_copy(
                src_ref=part.at[k], dst_ref=landed.at[r, chip], send_sem=part_send, recv_sem=part_recv.at[r],
                device_id={"narrow": row * 2 + core, "wide": to_wide}, device_id_type=MESH).start()

    for i in range(cuts):
        swaps[i].wait_recv()
        total = (kept[:, i * step:(i + 1) * step] + theirs[i]).astype(BF16)
        for k in range(pieces):
            q, j = k // cols, k % cols - i * step // LANES
            if 0 <= j < step // LANES:
                part[k] = total[q * tall:(q + 1) * tall, j * LANES:(j + 1) * LANES]
                send_part(k)
    each(1, wide, send_block)
    wait_bytes(blocks.at[n, pl.ds(0, wide - 1)], in_recv)

    def send_blocks(a):
        pltpu.make_async_remote_copy(
            src_ref=blocks.at[n], dst_ref=blocks.at[n], send_sem=inx_send, recv_sem=inx_recv,
            device_id={"narrow": rem(n + a, narrow), "wide": w}, device_id_type=MESH).start()

    each(1, narrow, send_blocks)
    hid_ref[...] = hidden.astype(F32).T.astype(BF16)

    def finish(r):
        own = owned[r]
        landed[r, chip] = part[own]
        wait_bytes(landed.at[r, pl.ds(0, chips - 1)], part_recv.at[r])
        reduced = jnp.sum(landed[r].astype(F32), axis=0)
        at = pl.ds(pl.multiple_of(core * half + rem(own, cols) * LANES, LANES), LANES)
        res[core, own] = (reduced + bias_ref[:, at]).astype(BF16)

        def send_res(to, a, b):
            pltpu.make_async_remote_copy(
                src_ref=res.at[core, own], dst_ref=res.at[core, own], send_sem=res_send.at[r],
                recv_sem=res_recv, device_id=to, device_id_type=MESH).start()

        peers(send_res)

    for r in range(rounds):
        pl.when(held[r])(functools.partial(finish, r))

    by_count(lambda count: wait_bytes(res.at[core, pl.ds(0, pieces - count)], res_recv))
    last = pltpu.make_async_remote_copy(
        src_ref=res.at[core], dst_ref=res.at[core], send_sem=rx_send, recv_sem=rx_recv,
        device_id=partner, device_id_type=MESH)
    last.start()
    first = assembled(core)
    dec_ref[...] = jnp.dot(hid_ref[...], first, preferred_element_type=F32).astype(BF16)
    back_ref[...] = lax.dot_general(first, w_ref[1], (((1,), (1,)), ((), ())), preferred_element_type=F32)

    wait_bytes(blocks.at[pl.ds(0, narrow - 1)], inx_recv)
    for a in range(narrow):
        for b in range(wide):
            whole[b * block_rows:(b + 1) * block_rows, a * block_cols:(a + 1) * block_cols] = (
                blocks[a, b].astype(F32))
    cent_ref[...] = (whole[...] - bias_ref[...]).T.astype(BF16)
    for swap in swaps:
        swap.wait_send()
    wait_bytes(blocks.at[n, pl.ds(0, wide - 1)], in_send)
    wait_bytes(blocks.at[pl.ds(0, narrow - 1)], inx_send)

    by_count(lambda count: wait_bytes(part.at[pl.ds(0, pieces - count)], part_send))
    for r in range(rounds):
        pl.when(held[r])(functools.partial(
            wait_bytes, landed.at[r, pl.ds(0, chips - 1)], res_send.at[r]))
    last.wait()
    resid_ref[...] = assembled(other)


def gradients(hid_ref, resid_ref, cent_ref, dec_ref, back_ref, pre_ref, w_ref, enc_hbm, dec_hbm,
              enc, dec, enc_sem, dec_sem):
    core = rem(lax.axis_index("narrow"), 2)
    half = resid_ref.shape[1]

    def columns(h):
        return pl.ds(pl.multiple_of(h * half, LANES), half)

    copies = [pltpu.make_async_copy(dec_ref, dec_hbm.at[:, columns(core)], dec_sem.at[0])]
    copies[0].start()
    backward = back_ref[...] + lax.dot_general(
        resid_ref[...], w_ref[:, columns(1 - core)], (((1,), (1,)), ((), ())), preferred_element_type=F32)
    masked = jnp.where(pre_ref[...].astype(F32) > 0, backward, 0.0).astype(BF16)
    dec[...] = jnp.dot(hid_ref[...], resid_ref[...], preferred_element_type=F32).astype(BF16)
    copies.append(pltpu.make_async_copy(dec, dec_hbm.at[:, columns(1 - core)], dec_sem.at[1]))
    copies[1].start()
    cuts = enc_sem.shape[0]
    step = enc.shape[0] // cuts
    for i in range(cuts):
        span = slice(i * step, (i + 1) * step)
        enc[span, :] = jnp.dot(
            cent_ref[span, :], masked, preferred_element_type=F32).astype(BF16)
        copies.append(pltpu.make_async_copy(enc.at[span, :], enc_hbm.at[span, :], enc_sem.at[i]))
        copies[-1].start()
    for copy in copies:
        copy.wait()


def shards(narrow, wide, inputs, decoder_bias, preactivations, decoder_weight):
    rows, features = preactivations.shape
    width = decoder_weight.shape[1]
    half, chips = width // 2, (narrow // 2) * wide
    cols = half // LANES
    groups = 1
    while cols * groups * 2 <= chips and rows % (groups * 2 * 16) == 0:
        groups *= 2
    pieces, tall = cols * groups, rows // groups
    cuts = 3 if cols % 3 == 0 else 1
    rounds = -(-pieces // (narrow // 2 * (wide // 2)))
    vmem, hbm = pl.BlockSpec(memory_space=pltpu.VMEM), pl.BlockSpec(memory_space=pltpu.HBM)
    dma = pltpu.SemaphoreType.DMA
    kept = pl.pallas_call(
        functools.partial(exchange, narrow, wide, pieces),
        out_shape=(jax.ShapeDtypeStruct((rows, half), BF16),
                   jax.ShapeDtypeStruct((width, rows), BF16),
                   jax.ShapeDtypeStruct((features, rows), BF16),
                   jax.ShapeDtypeStruct((features, half), BF16),
                   jax.ShapeDtypeStruct((rows, features), F32)),
        in_specs=[hbm] * 4,
        out_specs=(vmem,) * 5,
        scratch_shapes=[
            pltpu.VMEM((2, features, half), BF16),
            pltpu.VMEM(inputs.shape, BF16),
            pltpu.VMEM((rows, features), BF16),
            pltpu.VMEM((width,), F32),
            pltpu.VMEM((1, width), F32),
            pltpu.VMEM((8, width), F32),
            pltpu.VMEM((narrow, wide) + inputs.shape, BF16),
            pltpu.VMEM((rows, width), F32),
            pltpu.VMEM((cuts, rows, half // cuts), F32),
            pltpu.VMEM((rows, half), F32),
            pltpu.VMEM((cuts, rows, half // cuts), F32),
            pltpu.VMEM((pieces, tall, LANES), BF16),
            pltpu.VMEM((rounds, chips, tall, LANES), BF16),
            pltpu.VMEM((2, pieces, tall, LANES), BF16),
            dma((2,)),
        ] + [dma] * 7 + [dma((cuts,)), dma((cuts,)), dma, dma((rounds,)), dma((rounds,)), dma, dma, dma],
        compiler_params=pltpu.CompilerParams(
            collective_id=0, has_side_effects=True, vmem_limit_bytes=32 * 2**20),
        name="exchange",
    )(*(pltpu.with_memory_space_constraint(x, pltpu.HBM)
        for x in (inputs, decoder_bias, preactivations, decoder_weight)))
    resid, centered, hidden, decoder, backward = kept
    return pl.pallas_call(
        gradients,
        out_shape=(jax.ShapeDtypeStruct((width, features), BF16),
                   jax.ShapeDtypeStruct((features, width), BF16)),
        in_specs=[vmem] * 7,
        out_specs=(hbm, hbm),
        scratch_shapes=[
            pltpu.VMEM((width, features), BF16),
            pltpu.VMEM((features, half), BF16),
            dma((3,)), dma((2,)),
        ],
        compiler_params=pltpu.CompilerParams(vmem_limit_bytes=32 * 2**20),
        name="gradients",
    )(hidden, resid, centered, decoder, backward, preactivations, decoder_weight)


def solution(mesh):
    placed = (P("wide", "narrow"), P(), P(None, ("narrow", "wide")), P(("narrow", "wide"), None))
    return jax.shard_map(
        functools.partial(shards, mesh.shape["narrow"], mesh.shape["wide"]),
        mesh=mesh,
        in_specs=placed,
        out_specs=(P(None, ("narrow", "wide")), P(("narrow", "wide"), None)),
        check_vma=False,
    )
```
